512 devices in a mesh: sec: 8 (over x, core), own: 32 (over y_hi, z), tile: 2 (over y_lo).
Axes of the slice: x: 4, y: 8 (y_hi: 4, y_lo: 2; y = y_hi * 2 + y_lo), z: 8, core: 2. Of those that a mesh axis runs over, the one named last changes fastest.
Arguments:
- couple: bfloat16 [4096, 3, 256, 256], P(('sec', 'own', 'tile')), may hold values from -1.5 to 1.5
- factors: bfloat16 [4096, 256, 256], P(('sec', 'own', 'tile')), as said below
- top_reflect: bfloat16 [4096, 64, 64], P(('sec', 'own', 'tile')), as said below
- wy_factor: bfloat16 [4096, 256, 64], P(('sec', 'own', 'tile')), may hold values from -0.375 to 0.375
- neighbour_ids: int32 [4096, 3], P(('sec', 'own', 'tile')), may hold values from 0 to 4095, as said below
- kept_rank: int32 [4096], P(('sec', 'own', 'tile')), may hold values from 8 to 64, as said below
- merge_map: int32 [4096, 3], P(('sec', 'own', 'tile')), may hold values from 0 to 31, all different within a row; in each aligned block of 8 rows (0 to 7, 8 to 15, ...) at most 2 rows name the same one
Outputs:
- merged: bfloat16 [8, 32, 64, 256], P('sec', 'own', None, 'tile')
The draws below stay inside these ranges and needn't reach their ends.
Inputs may be any that keep to these rules, and one draw needn't show every extreme that they name: factors[c] is lower triangular with a positive diagonal. top_reflect[c] is lower triangular with a unit diagonal. neighbour_ids[c, j] lies on the device with c's sec and tile index whose own index is one lower (j % 3 == 0) or one higher (j % 3 == 1) than c's, or on the device with c's own and tile index whose sec index is one away (j % 3 == 2); where the first choice leaves the axis, the other side is taken; both ends of the range are reached in every draw. `kept_rank`: a multiple of 8; on every device at least one cluster keeps 64 rows. `merge_map`: a cluster's 3 blocks go to different merged blocks; at most 2 blocks of one device go to one merged block, and some device sends exactly 2 to one.
All inputs are finite; a program needn't handle non-finite values.
Results may differ from the reference program's by a relative error of at most 0.01.
Values may be sent and summed in bfloat16 or wider, within the bound.
A program may use at most 64 MiB of HBM per device.

```python
import math
import jax
import jax.numpy as jnp
import numpy as np
from jax import lax

CW = 256
KMAX = 64
NB = 3
CL = 8
CLUSTERS = 4096
CAP = 2
N_SEC = 8
N_OWN = 32
N_TILE = 2
DEVICES = 512


def draw_factors(key, part):
    first, second = jax.random.split(key)
    strict = jnp.tril(jnp.ones((CW, CW), jnp.float32), -1)
    diagonal = jax.random.uniform(first, (CLUSTERS, CW), jnp.float32, 0.6, 1.4)
    below = jax.random.normal(second, (CLUSTERS, CW, CW), jnp.float32)
    eye_full = jnp.eye(CW, dtype=jnp.float32)
    result = below * strict * (0.7 / math.sqrt(CW)) + eye_full[None, :, :] * diagonal[:, :, None]
    return result.astype(jnp.bfloat16)


def draw_top_reflect(key, part):
    strict = jnp.tril(jnp.ones((KMAX, KMAX), jnp.float32), -1)
    below = jax.random.normal(key, (CLUSTERS, KMAX, KMAX), jnp.float32)
    result = below * strict * (1.0 / math.sqrt(KMAX)) + jnp.eye(KMAX, dtype=jnp.float32)[None, :, :]
    return result.astype(jnp.bfloat16)


def draw_neighbour_ids(key, part):
    first, second = jax.random.split(key)
    cluster = jnp.arange(CLUSTERS, dtype=jnp.int32)
    device = cluster // CL
    tile_pos = device % N_TILE
    own_pos = device // N_TILE % N_OWN
    sec_pos = device // (N_TILE * N_OWN)
    direction = jax.random.randint(first, (CLUSTERS, NB), 0, 2).astype(jnp.int32) * 2 - 1
    lower = jnp.where(own_pos > 0, own_pos - 1, own_pos + 1)
    upper = jnp.where(own_pos < N_OWN - 1, own_pos + 1, own_pos - 1)
    kind = jnp.arange(NB, dtype=jnp.int32)[None, :] % 3
    side = sec_pos[:, None] + direction
    side = jnp.where(side < 0, 1, side)
    side = jnp.where(side > N_SEC - 1, N_SEC - 2, side)
    own_new = jnp.where(kind == 0, lower[:, None], jnp.where(kind == 1, upper[:, None], own_pos[:, None]))
    sec_new = jnp.where(kind == 2, side, sec_pos[:, None])
    local = jax.random.randint(second, (CLUSTERS, NB), 0, CL).astype(jnp.int32)
    local = local.at[N_TILE * CL, 0].set(0)
    local = local.at[CLUSTERS - 1 - CL * N_TILE, 1].set(CL - 1)
    dev_new = (sec_new * N_OWN + own_new) * N_TILE + tile_pos[:, None]
    return (dev_new * CL + local).astype(jnp.int32)


def draw_kept_rank(key, part):
    first, second = jax.random.split(key)
    base = 8 * jax.random.randint(first, (CLUSTERS,), 1, KMAX // 8 + 1).astype(jnp.int32)
    chosen = jax.random.randint(second, (CLUSTERS // CL,), 0, CL).astype(jnp.int32)
    position = jnp.arange(CLUSTERS, dtype=jnp.int32) % CL
    return jnp.where(position == jnp.repeat(chosen, CL), KMAX, base).astype(jnp.int32)


def shard_levels(own_key, shape, shards, low, top_value):
    factor_of, own = 1.0, jax.random.fold_in(own_key, 6)
    for dim, parts in shards:
        heights = jnp.exp(jax.random.uniform(jax.random.fold_in(own, dim), (parts,), jnp.float32, low / len(shards), top_value / len(shards)))
        factor_of = factor_of * jnp.repeat(heights, shape[dim] // parts).reshape([-1 if axis == dim else 1 for axis in range(len(shape))])
    return factor_of


def shared_out(own_key, own, number, rows, number_of, top, most, skew):
    ranking = jax.random.permutation(own_key, number_of)
    crowded, ordinary = load_shares(number_of, rows * top, most, skew, True), load_shares(number_of, rows * top, most, skew, False)
    places = jnp.arange(number_of)

    def named(sizes, rotation):
        used = int((sizes > 0).sum())
        fixed = max(1, used // 4)
        shifted = fixed + (places - fixed + rotation * (used - fixed)) % max(1, number_of - fixed)
        return jnp.zeros((number_of,), jnp.int32).at[ranking[jnp.where(places < fixed, places, shifted)]].set(jnp.asarray(sizes, jnp.int32))

    sizes = jnp.where(number % 4 == 0, named(crowded, number // 4), named(ordinary, number - number // 4 - 1))
    mixed = jax.random.permutation(jax.random.fold_in(own, 3), number_of)
    source_of, receiver = mixed[0:number_of // 2 * 2:2], mixed[1:number_of // 2 * 2:2]
    margin = jnp.minimum(sizes[source_of] - 1, most - sizes[receiver]) // 2
    margin = jnp.where((source_of == ranking[0]) | (receiver == ranking[0]) | (sizes[receiver] == 0), 0, jnp.maximum(margin, 0))
    shifted = jax.random.randint(jax.random.fold_in(own, 4), (number_of // 2,), 0, 1 << 20) % (margin + 1)
    sizes = sizes.at[source_of].add(-shifted).at[receiver].add(shifted)
    members = jnp.searchsorted(jnp.cumsum(sizes), jnp.arange(rows * top), side="right").astype(jnp.int32)
    grid = members.reshape(top, rows).T
    grid = grid[jax.random.permutation(jax.random.fold_in(own, 1), rows)]
    rotation = jax.random.randint(jax.random.fold_in(own, 2), (rows, 1), 0, top)
    return jnp.take_along_axis(grid, (jnp.arange(top)[None, :] + rotation) % top, axis=1)


def load_shares(number_of, total, bound, skew, full):
    loads = [(1 << 20) // math.isqrt(standing ** skew) + 1 for standing in range(1, number_of + 1)]
    largest = bound if full else min(bound, max(-(-total // number_of), total * loads[0] // sum(loads)))
    least = 1 if total - largest >= number_of - 1 else 0
    given, surplus = [largest] + [least] * (number_of - 1), total - largest - least * (number_of - 1)
    while surplus > 0:
        free = [i for i in range(1, number_of) if given[i] < largest] or [i for i in range(1, number_of) if given[i] < bound]
        mass, remaining = sum([loads[i] for i in free]), surplus
        for i in free:
            more = min(bound - given[i], max(1, remaining * loads[i] // mass), surplus)
            given[i] = given[i] + more
            surplus = surplus - more
    return np.array(given)


def bell_draw(stream_key, shape, width, bound, pieces=(), kind=jnp.bfloat16):
    entries = width * jax.random.normal(stream_key, shape, jnp.float32)
    if pieces:
        entries = entries * shard_levels(stream_key, shape, pieces, -0.22, 0.18)
    return jnp.clip(entries, -bound, bound).astype(kind)


def setup_inputs(seed: int = 0) -> dict:
    key_of = jax.random.split(jax.random.key(seed), 8)
    couple = bell_draw(key_of[0], (CLUSTERS, NB, CW, CW), 16 ** -0.5, 1.5, ((0, 512),))
    factors = draw_factors(jax.random.fold_in(key_of[7], 71), 0)
    top_reflect = draw_top_reflect(jax.random.fold_in(key_of[7], 71), 0)
    wy_factor = bell_draw(key_of[3], (CLUSTERS, CW, KMAX), CW ** -0.5, 0.375, ((0, 512),))
    neighbour_ids = draw_neighbour_ids(jax.random.fold_in(key_of[7], 71), 0)
    kept_rank = draw_kept_rank(jax.random.fold_in(key_of[7], 71), 0)
    merge_map_keys = jax.random.split(jax.random.fold_in(key_of[6], 1), CLUSTERS // CL)
    merge_map_turns = jax.random.permutation(jax.random.fold_in(key_of[6], 3), CLUSTERS // CL)
    merge_map = jax.vmap(lambda own, number: shared_out(jax.random.fold_in(key_of[6], 2), own, number, CL, N_OWN, NB, CAP, 2))(merge_map_keys, merge_map_turns).reshape((CLUSTERS, NB))
    return {"couple": couple, "factors": factors, "top_reflect": top_reflect, "wy_factor": wy_factor, "neighbour_ids": neighbour_ids, "kept_rank": kept_rank, "merge_map": merge_map}


def coarse_rows(couple_dev, factor_dev, near_factors, reflect_dev, wy_dev, rank_dev):
    left = jnp.einsum("cik,cjkl->cjil", factor_dev.astype(jnp.float32), couple_dev.astype(jnp.float32)).astype(jnp.bfloat16)
    scaled = jnp.einsum("cjil,cjml->cjim", left.astype(jnp.float32), near_factors.astype(jnp.float32)).astype(jnp.bfloat16)
    projected = jnp.einsum("cia,cjim->cjam", wy_dev.astype(jnp.float32), scaled.astype(jnp.float32)).astype(jnp.bfloat16)
    leading = scaled[:, :, :KMAX, :].astype(jnp.float32)
    coarse = leading - jnp.einsum("cab,cjbm->cjam", reflect_dev.astype(jnp.float32), projected.astype(jnp.float32))
    live = jnp.arange(KMAX, dtype=jnp.int32)[None, :] < rank_dev[:, None]
    return jnp.where(live[:, None, :, None], coarse, 0.0).astype(jnp.bfloat16)


def reference(couple, factors, top_reflect, wy_factor, neighbour_ids, kept_rank, merge_map):
    def by_device(array):
        return array.reshape((DEVICES, CL) + array.shape[1:])

    inputs = (by_device(couple), by_device(factors), by_device(top_reflect), by_device(wy_factor),
              by_device(neighbour_ids), by_device(kept_rank), by_device(merge_map),
              jnp.arange(DEVICES, dtype=jnp.int32))

    def step_device(total, item):
        couple_dev, factor_dev, reflect_dev, wy_dev, near_ids, rank_dev, map_dev, device = item
        near_factors = factors[near_ids]
        coarse = coarse_rows(couple_dev, factor_dev, near_factors, reflect_dev, wy_dev, rank_dev)
        section = device // (N_OWN * N_TILE)
        target = (section * N_OWN + map_dev).reshape(-1).astype(jnp.int32)
        total = total.at[target].add(coarse.reshape((-1, KMAX, CW)).astype(jnp.float32))
        return total, None

    start_total = jnp.zeros((N_SEC * N_OWN, KMAX, CW), jnp.float32)
    total, _ = lax.scan(step_device, start_total, inputs)
    return total.reshape(N_SEC, N_OWN, KMAX, CW).astype(jnp.bfloat16)
```

```python
import jax
import jax.numpy as jnp
from jax import lax
from jax.experimental import pallas as pl
from jax.experimental.pallas import tpu as pltpu
from jax.sharding import PartitionSpec as P

MESH = pl.DeviceIdType.MESH
F32 = jnp.float32
BF16 = jnp.bfloat16
CL, NB, CW, K = 8, 3, 256, 64
HALF = CW // 2
RING = 8
OWNERS = 32
SECTIONS = 8
PER_SECTION = 512
EMPTY = 32


def dot(a, b):
    return lax.dot_general(a, b, (((1,), (0,)), ((), ())), preferred_element_type=F32)


def dot_t(a, b):
    return lax.dot_general(a, b, (((1,), (1,)), ((), ())), preferred_element_type=F32)


def kernel(couple, factors, reflect, wy, nid, rank, mmap, out,
           couple_v, fac, refl_v, wy_v, sec_top, sec_bot, zs, zr, tab_s, tab_v, tab, coarse, total,
           za3, za4, zad, zas, zat, ya3, ya4, yad, yas, yat, pa, pb, ra, rb,
           load_sem, ss, rs):
    sec, own, tile = lax.axis_index("sec"), lax.axis_index("own"), lax.axis_index("tile")
    z, y = lax.rem(own, RING), (own // RING) * 2 + tile

    def zdev(d):
        return {"own": (own // RING) * RING + lax.rem(z + d + RING, RING)}

    def ydev(d):
        to = lax.rem(y + d + RING, RING)
        return {"own": (to // 2) * RING + z, "tile": lax.rem(to, 2)}

    def sdev(d):
        return {"sec": lax.rem(sec + d + SECTIONS, SECTIONS)}

    has_low, has_up = own > 0, own < OWNERS - 1
    low = jnp.where(has_low, own - 1, own + 1)
    up = jnp.where(has_up, own + 1, own - 1)

    loads = [pltpu.make_async_copy(factors, fac, load_sem.at[0]),
             pltpu.make_async_copy(wy, wy_v, load_sem.at[1]),
             pltpu.make_async_copy(reflect, refl_v, load_sem.at[2])]
    for part in range(2):
        at = pl.ds(part * 4, 4)
        loads.append(pltpu.make_async_copy(couple.at[at], couple_v.at[at], load_sem.at[3 + part]))
    for copy in loads:
        copy.start()

    barrier = pltpu.get_barrier_semaphore()

    def greet(to):
        pl.semaphore_signal(barrier, inc=1, device_id=to, device_id_type=MESH)

    greet(sdev(1))
    greet(sdev(-1))

    @pl.when(has_low)
    def _():
        greet({"own": own - 1})

    @pl.when(has_up)
    def _():
        greet({"own": own + 1})

    for d in (1, -1, 2, -2, 3, -3, 4):
        greet(zdev(d))
        greet(ydev(d))

    lane = lax.broadcasted_iota(jnp.int32, (8, 128), 1)
    row = lax.broadcasted_iota(jnp.int32, (8, 128), 0)

    def table(groups):
        first = jnp.full((8, 128), EMPTY, jnp.int32)
        second = jnp.full((8, 128), EMPTY, jnp.int32)
        local = jnp.zeros((8, 128), jnp.int32)
        for j, base, wanted in groups:
            for c in range(CL):
                hit = lane == mmap[j, c]
                if wanted is not None:
                    hit = hit & wanted
                second = jnp.where(hit & (first != EMPTY), base + c, second)
                first = jnp.where(hit & (first == EMPTY), base + c, first)
                local = jnp.where(lane == base + c, nid[j, c] & (CL - 1), local)
        return jnp.where(row == 0, first, jnp.where(row == 1, second, local))

    at_low_end = jnp.full((8, 128), own, jnp.int32) == 0
    at_up_end = jnp.full((8, 128), own, jnp.int32) == OWNERS - 1
    tab_s[0] = table([(0, 8, None), (1, 24, at_up_end)])
    tab_s[1] = table([(1, 16, None), (0, 24, at_low_end)])
    tab_v[2] = table([(2, 0, None)])
    nothing = jnp.where(row < 2, EMPTY, 0)

    @pl.when(jnp.logical_not(has_low))
    def _():
        tab_v[0] = nothing

    @pl.when(jnp.logical_not(has_up))
    def _():
        tab_v[1] = nothing

    coarse[EMPTY] = jnp.zeros((K, CW), F32)
    edges = has_low.astype(jnp.int32) + has_up.astype(jnp.int32)
    pl.semaphore_wait(barrier, 2 + 14 + edges)

    count = [0]

    def remote(src, dst, to):
        i = count[0]
        count[0] += 1
        return pltpu.make_async_remote_copy(src_ref=src, dst_ref=dst, send_sem=ss.at[i], recv_sem=rs.at[i],
                                            device_id=to, device_id_type=MESH)

    sends = []
    for side, d in ((0, 1), (1, -1)):
        at = pl.ds(side * CL, CL)
        sends.append(remote(factors.at[:, pl.ds(HALF, HALF), :], sec_bot.at[at], sdev(d)))
        sends.append(remote(factors.at[:, pl.ds(0, HALF), pl.ds(0, HALF)], sec_top.at[at], sdev(d)))
    for copy in sends:
        copy.start()
    sec_copies = list(sends)
    to_low = remote(tab_s.at[0], tab_v.at[1], {"own": low})
    to_up = remote(tab_s.at[1], tab_v.at[0], {"own": up})

    @pl.when(has_low)
    def _():
        to_low.start()

    @pl.when(has_up)
    def _():
        to_up.start()

    base_sem = count[0]
    count[0] += 6
    for copy in loads[:3]:
        copy.wait()
    r_iota = lax.broadcasted_iota(jnp.int32, (K, CW), 0)
    c_iota = lax.broadcasted_iota(jnp.int32, (K, CW), 1)
    eye = jnp.where(r_iota == c_iota, 1.0, 0.0)
    z_copies = []
    low_group = jnp.where(has_low, 0, 2)
    up_group = jnp.where(has_up, 1, 2)
    for part in range(2):
        loads[3 + part].wait()
        tops = []
        for c in range(part * 4, part * 4 + 4):
            t = eye - dot(refl_v[c], wy_v[c])
            t = jnp.where(r_iota < rank[c], t, 0.0).astype(BF16)
            tops.append(dot(t, fac[c]).astype(BF16))
        for j in range(NB):
            for c in range(part * 4, part * 4 + 4):
                zs[j, c] = dot(tops[c - part * 4], couple_v[c, j]).astype(BF16)
            if j < 2:
                group = (low_group, up_group)[j]
                at = pl.ds(part * 4, 4)
                copy = pltpu.make_async_remote_copy(
                    src_ref=zs.at[j, at], dst_ref=zr.at[group, at], send_sem=ss.at[base_sem + 2 * j + part],
                    recv_sem=rs.at[base_sem + 2 * group + part], device_id={"own": (low, up)[j]}, device_id_type=MESH)
                copy.start()
                z_copies.append(copy)

    @pl.when(has_low)
    def _():
        to_low.wait_send()
        to_up_like = to_up
        to_up_like.wait_recv()

    @pl.when(has_up)
    def _():
        to_up.wait_send()
        to_low.wait_recv()

    tab_copy = pltpu.make_async_copy(tab_v, tab, load_sem.at[5])
    tab_copy.start()
    tab_copy.wait()

    for copy in sec_copies:
        copy.wait()
    for c in range(CL):
        n = nid[2, c]
        at = (n & (CL - 1)) + jnp.where(n // PER_SECTION > sec, CL, 0)
        coarse[c, :, pl.ds(0, HALF)] = dot_t(zs[2, c, :, pl.ds(0, HALF)], sec_top[at])
        coarse[c, :, pl.ds(HALF, HALF)] = dot_t(zs[2, c], sec_bot[at])

    def landed(group, part):
        at = pl.ds(part * 4, 4)
        pltpu.make_async_remote_copy(
            src_ref=zs.at[0, at], dst_ref=zr.at[group, at], send_sem=ss.at[base_sem], recv_sem=rs.at[base_sem + 2 * group + part],
            device_id={"own": low}, device_id_type=MESH).wait_recv()

    def finish(group, base, side, part):
        for c in range(part * 4, part * 4 + 4):
            at = tab[side, 2, base + c]
            coarse[base + c] = dot_t(zr[group, c], fac[at])

    for part in range(2):
        @pl.when(has_up)
        def _():
            landed(0, part)
            finish(0, 8, 1, part)

        @pl.when(has_low)
        def _():
            landed(1, part)
            finish(1, 16, 0, part)

    @pl.when(own == 1)
    def _():
        for part in range(2):
            landed(2, part)
            finish(2, 24, 0, part)

    @pl.when(own == OWNERS - 2)
    def _():
        for part in range(2):
            landed(2, part)
            finish(2, 24, 1, part)

    for yh in range(4):
        def gather(zz, _):
            m = yh * RING + zz
            acc = coarse[tab[0, 0, m]] + coarse[tab[0, 1, m]]
            acc = acc + coarse[tab[1, 0, m]] + coarse[tab[1, 1, m]]
            acc = acc + coarse[tab[2, 0, m]] + coarse[tab[2, 1, m]]
            total[yh, zz] = acc.astype(BF16)
            return 0

        lax.fori_loop(0, RING, gather, 0)

    def zpiece(d, part=None):
        rows = pl.ds(0, 4) if part is None else pl.ds(2 * part, 2)
        return total.at[rows, lax.rem(z + d + RING, RING), pl.ds(0, 32), :]

    def ypiece(d, part=None):
        to = lax.rem(y + d + RING, RING)
        rows = pl.ds(0, 8) if part is None else pl.ds(4 * part, 4)
        return total.at[to // 2, rows, pl.ds(32, 32), pl.ds(pl.multiple_of(lax.rem(to, 2) * HALF, HALF), HALF)]

    axes = ((zpiece, zdev, za3, za4, zad, zas, zat, 2), (ypiece, ydev, ya3, ya4, yad, yas, yat, 4))
    fours, threes, ones = [], [], []
    for piece, dev, b3, b4, bd, _, _, _ in axes:
        for side, s in ((0, 1), (1, -1)):
            fours.append(remote(piece(4 * s, side), b4.at[side], dev(2 * s)))
            threes.append(remote(piece(3 * s), b3.at[side], dev(s)))
            ones.append(remote(piece(s), bd.at[side], dev(s)))
    for copy in fours + threes + ones:
        copy.start()
    twos = []
    for a, (piece, dev, b3, b4, bd, bs, bt, half) in enumerate(axes):
        for side, s in ((0, 1), (1, -1)):
            i = 2 * a + side
            fours[i].wait_recv()
            threes[i].wait_recv()
            near = pl.ds(half * side, half)
            far = pl.ds(half * (1 - side), half)
            mine = piece(2 * s)
            b3s = b3.at[side]
            bts = bt.at[side]
            bts[near] = (mine[near].astype(F32) + b3s[near].astype(F32) + b4[side].astype(F32)).astype(BF16)
            bts[far] = (mine[far].astype(F32) + b3s[far].astype(F32)).astype(BF16)
            copy = remote(bts, bs.at[side], dev(2 * s))
            copy.start()
            twos.append(copy)
    for copy in ones + twos:
        copy.wait_recv()
    sum_a = zpiece(0)[...].astype(F32)
    sum_b = ypiece(0)[...].astype(F32)
    for side in range(2):
        sum_a = sum_a + zad[side].astype(F32) + zas[side].astype(F32)
        sum_b = sum_b + yad[side].astype(F32) + yas[side].astype(F32)
    for part in range(2):
        for yh in range(4):
            pa[2 * yh + part] = sum_a[yh, :, part * HALF:(part + 1) * HALF].astype(BF16)
    pb[...] = sum_b.astype(BF16)

    last = []
    for d in (4, 3, 5, 2, 6, 1, 7):
        last.append(remote(pa.at[lax.rem(y + d, RING)], ra.at[d - 1], ydev(d)))
        last.append(remote(pb.at[lax.rem(z + d, RING)], rb.at[d - 1], zdev(d)))
    for copy in last:
        copy.start()
    for copy in last:
        copy.wait_recv()
    done_a, done_b = pa[y].astype(F32), pb[z].astype(F32)
    for d in range(RING - 1):
        done_a = done_a + ra[d].astype(F32)
        done_b = done_b + rb[d].astype(F32)
    out[0, 0, pl.ds(0, 32), :] = done_a.astype(BF16)
    out[0, 0, pl.ds(32, 32), :] = done_b.astype(BF16)
    for copy in z_copies + fours + threes + ones + twos + last:
        copy.wait_send()


def on_device(couple, factors, top_reflect, wy_factor, neighbour_ids, kept_rank, merge_map):
    hbm, smem, vmem = (pl.BlockSpec(memory_space=s) for s in (pl.ANY, pltpu.SMEM, pltpu.VMEM))
    v = lambda *shape: pltpu.VMEM(shape, BF16)
    return pl.pallas_call(
        kernel,
        name="merge_level",
        out_shape=jax.ShapeDtypeStruct((1, 1, K, HALF), BF16),
        in_specs=[hbm, hbm, hbm, hbm, smem, smem, smem],
        out_specs=vmem,
        scratch_shapes=[
            v(CL, NB, CW, CW), v(CL, CW, CW), v(CL, K, K), v(CL, K, CW),
            v(2 * CL, HALF, HALF), v(2 * CL, HALF, CW),
            v(NB, CL, K, CW), v(3, CL, K, CW),
            pltpu.VMEM((2, 8, 128), jnp.int32), pltpu.VMEM((3, 8, 128), jnp.int32), pltpu.SMEM((3, 8, 128), jnp.int32),
            pltpu.VMEM((EMPTY + 1, K, CW), F32), v(4, RING, K, CW),
            v(2, 4, 32, CW), v(2, 2, 32, CW), v(2, 4, 32, CW), v(2, 4, 32, CW), v(2, 4, 32, CW),
            v(2, 8, 32, HALF), v(2, 4, 32, HALF), v(2, 8, 32, HALF), v(2, 8, 32, HALF), v(2, 8, 32, HALF),
            v(8, 32, HALF), v(8, 32, HALF), v(7, 32, HALF), v(7, 32, HALF),
            pltpu.SemaphoreType.DMA((6,)), pltpu.SemaphoreType.DMA((42,)), pltpu.SemaphoreType.DMA((42,)),
        ],
        compiler_params=pltpu.CompilerParams(collective_id=0, has_side_effects=True, vmem_limit_bytes=62 << 20),
    )(couple, factors, top_reflect, wy_factor.transpose(0, 2, 1), neighbour_ids.T, kept_rank, merge_map.T)


def solution(mesh):
    own = ("sec", "own", "tile")
    in_specs = (P(own, None, None, None), P(own, None, None), P(own, None, None), P(own, None, None),
                P(own, None), P(own), P(own, None))
    return jax.shard_map(on_device, mesh=mesh, in_specs=in_specs, out_specs=P("sec", "own", None, "tile"), check_vma=False)
```

```python
import jax
import jax.numpy as jnp
from jax import lax
from jax.experimental import pallas as pl
from jax.experimental.pallas import tpu as pltpu
from jax.sharding import PartitionSpec as P

MESH = pl.DeviceIdType.MESH
F32 = jnp.float32
BF16 = jnp.bfloat16
CL, NB, CW, K = 8, 3, 256, 64
HALF = CW // 2
RING = 8
OWNERS = 32
SECTIONS = 8
PER_SECTION = 512
PARTS = 4
PER = CL // PARTS
SEMS = 72
EMPTY = 32


def dot(a, b):
    return lax.dot_general(a, b, (((1,), (0,)), ((), ())), preferred_element_type=F32)


def dot_t(a, b):
    return lax.dot_general(a, b, (((1,), (1,)), ((), ())), preferred_element_type=F32)


def kernel(couple, factors, reflect, wy, nid_h, rank_h, mmap_h, out,
           nid, rank, mmap, couple_v, fac, refl_v, wy_v, pack, diag, sec_b, sec_u, sec_d, zs, zr, fw, tab_s, tab_v, tab, coarse, total,
           za3, za4, zad, zas, zat, ya3, ya4, yad, yas, yat, pa, pb, ra, rb,
           load_sem, ss, rs):
    sec, own, tile = lax.axis_index("sec"), lax.axis_index("own"), lax.axis_index("tile")
    z, y = lax.rem(own, RING), (own // RING) * 2 + tile

    def zdev(d):
        return {"own": (own // RING) * RING + lax.rem(z + d + RING, RING)}

    def ydev(d):
        to = lax.rem(y + d + RING, RING)
        return {"own": (to // 2) * RING + z, "tile": lax.rem(to, 2)}

    def sdev(d):
        return {"sec": lax.rem(sec + d + SECTIONS, SECTIONS)}

    has_low, has_up = own > 0, own < OWNERS - 1
    low = jnp.where(has_low, own - 1, own + 1)
    up = jnp.where(has_up, own + 1, own - 1)

    ints = [pltpu.make_async_copy(a, b, load_sem.at[6 + i]) for i, (a, b) in enumerate(((mmap_h, mmap), (nid_h, nid), (rank_h, rank)))]
    loads = [pltpu.make_async_copy(factors, fac, load_sem.at[0]),
             pltpu.make_async_copy(wy, wy_v, load_sem.at[1]),
             pltpu.make_async_copy(reflect, refl_v, load_sem.at[2])]
    couples = []
    for part in range(PARTS):
        at = pl.ds(part * PER, PER)
        couples.append(pltpu.make_async_copy(couple.at[at], couple_v.at[at], load_sem.at[9 + part]))
    for copy in ints + loads + couples:
        copy.start()

    barrier = pltpu.get_barrier_semaphore()

    def greet(to):
        pl.semaphore_signal(barrier, inc=1, device_id=to, device_id_type=MESH)

    greet(sdev(1))
    greet(sdev(-1))

    @pl.when(has_low)
    def _():
        greet({"own": own - 1})

    @pl.when(has_up)
    def _():
        greet({"own": own + 1})

    for d in (1, -1, 2, -2, 3, -3, 4):
        greet(zdev(d))
        greet(ydev(d))

    for copy in ints:
        copy.wait()
    lane = lax.broadcasted_iota(jnp.int32, (8, 128), 1)
    row = lax.broadcasted_iota(jnp.int32, (8, 128), 0)

    def table(groups):
        first = jnp.full((8, 128), EMPTY, jnp.int32)
        second = jnp.full((8, 128), EMPTY, jnp.int32)
        local = jnp.zeros((8, 128), jnp.int32)
        for j, base, wanted in groups:
            for c in range(CL):
                hit = lane == mmap[j, c]
                if wanted is not None:
                    hit = hit & wanted
                second = jnp.where(hit & (first != EMPTY), base + c, second)
                first = jnp.where(hit & (first == EMPTY), base + c, first)
                local = jnp.where(lane == base + c, nid[j, c] & (CL - 1), local)
        return jnp.where(row == 0, first, jnp.where(row == 1, second, local))

    at_low_end = jnp.full((8, 128), own, jnp.int32) == 0
    at_up_end = jnp.full((8, 128), own, jnp.int32) == OWNERS - 1
    tab_s[0] = table([(0, 8, None), (1, 24, at_up_end)])
    tab_s[1] = table([(1, 16, None), (0, 24, at_low_end)])
    tab_v[2] = table([(2, 0, None)])
    nothing = jnp.where(row < 2, EMPTY, 0)

    @pl.when(jnp.logical_not(has_low))
    def _():
        tab_v[0] = nothing

    @pl.when(jnp.logical_not(has_up))
    def _():
        tab_v[1] = nothing

    coarse[EMPTY] = jnp.zeros((K, CW), F32)
    edges = has_low.astype(jnp.int32) + has_up.astype(jnp.int32)
    pl.semaphore_wait(barrier, 2 + 14 + edges)

    count = [0]

    def remote(src, dst, to):
        i = count[0]
        count[0] += 1
        return pltpu.make_async_remote_copy(src_ref=src, dst_ref=dst, send_sem=ss.at[i], recv_sem=rs.at[i],
                                            device_id=to, device_id_type=MESH)

    loads[0].wait()
    sec_copies = []
    for side, d in ((0, 1), (1, -1)):
        copy = remote(fac.at[:, pl.ds(HALF, HALF), pl.ds(0, HALF)], sec_b.at[pl.ds(side * CL, CL)], sdev(d))
        copy.start()
        sec_copies.append(copy)
    sq_r = lax.broadcasted_iota(jnp.int32, (HALF, HALF), 0)
    sq_c = lax.broadcasted_iota(jnp.int32, (HALF, HALF), 1)
    for c in range(CL):
        lower = fac[c, pl.ds(HALF, HALF), pl.ds(HALF, HALF)].astype(F32)
        diag[pl.ds(c, 1), :] = jnp.sum(jnp.where(sq_r == sq_c, lower, 0.0), axis=0, keepdims=True)
        upper = fac[c, pl.ds(0, HALF), pl.ds(0, HALF)].astype(F32)
        pack[c] = jnp.where(sq_r >= sq_c, upper, lower.T).astype(BF16)
    for side, d in ((0, 1), (1, -1)):
        at = pl.ds(side * CL, CL)
        for copy in (remote(pack, sec_u.at[at], sdev(d)), remote(diag, sec_d.at[at], sdev(d))):
            copy.start()
            sec_copies.append(copy)
    to_low = remote(tab_s.at[0], tab_v.at[1], {"own": low})
    to_up = remote(tab_s.at[1], tab_v.at[0], {"own": up})

    @pl.when(has_low)
    def _():
        to_low.start()

    @pl.when(has_up)
    def _():
        to_up.start()

    base_sem = count[0]
    count[0] += 3 * PARTS
    fw_sem = count[0]
    count[0] += 2
    on_sem = count[0]
    count[0] += 2
    for copy in loads[1:]:
        copy.wait()
    r_iota = lax.broadcasted_iota(jnp.int32, (K, CW), 0)
    c_iota = lax.broadcasted_iota(jnp.int32, (K, CW), 1)
    eye = jnp.where(r_iota == c_iota, 1.0, 0.0)
    low_group = jnp.where(has_low, 0, 2)
    up_group = jnp.where(has_up, 1, 2)
    cross_low = (z == 0) & has_low
    cross_up = (z == RING - 1) & has_up
    tops = []
    for c in range(CL):
        t = eye - dot(refl_v[c], wy_v[c])
        t = jnp.where(r_iota < rank[c], t, 0.0).astype(BF16)
        tops.append(dot(t, fac[c]).astype(BF16))
    z_sends = []

    def z_send(j, part):
        at = pl.ds(part * PER, PER)
        group = (low_group, up_group)[j]
        to = (low, up)[j]
        crossing = (cross_low, cross_up)[j]
        plain = pltpu.make_async_remote_copy(
            src_ref=zs.at[j, at], dst_ref=zr.at[group, at], send_sem=ss.at[base_sem + j * PARTS + part],
            recv_sem=rs.at[base_sem + group * PARTS + part], device_id={"own": to}, device_id_type=MESH)
        z_sends.append(plain)
        if part >= 2:
            plain.start()
            return
        by_way = pltpu.make_async_remote_copy(
            src_ref=zs.at[j, at], dst_ref=fw.at[pl.ds(part * PER, PER)], send_sem=ss.at[base_sem + j * PARTS + part],
            recv_sem=rs.at[fw_sem + part], device_id=zdev((-1, 1)[j]), device_id_type=MESH)

        @pl.when(crossing)
        def _():
            by_way.start()

        @pl.when(jnp.logical_not(crossing))
        def _():
            plain.start()

    for part in range(PARTS):
        couples[part].wait()
        for j in (1, 0, 2):
            for c in range(part * PER, part * PER + PER):
                zs[j, c] = dot(tops[c], couple_v[c, j]).astype(BF16)
            if j < 2:
                z_send(j, part)

    def send_on(group, to, part):
        at = pl.ds(part * PER, PER)
        return pltpu.make_async_remote_copy(
            src_ref=fw.at[at], dst_ref=zr.at[group, at], send_sem=ss.at[on_sem + part],
            recv_sem=rs.at[base_sem + group * PARTS + part], device_id={"own": to}, device_id_type=MESH)

    def fw_landed(part):
        at = pl.ds(part * PER, PER)
        pltpu.make_async_remote_copy(src_ref=zs.at[0, at], dst_ref=fw.at[at], send_sem=ss.at[base_sem], recv_sem=rs.at[fw_sem + part],
                                     device_id=zdev(1), device_id_type=MESH).wait_recv()

    def landed(group, part):
        at = pl.ds(part * PER, PER)
        pltpu.make_async_remote_copy(
            src_ref=zs.at[0, at], dst_ref=zr.at[group, at], send_sem=ss.at[base_sem], recv_sem=rs.at[base_sem + group * PARTS + part],
            device_id={"own": low}, device_id_type=MESH).wait_recv()

    on_up = (z == 0) & (own < OWNERS - RING)
    on_low = (z == RING - 1) & (own >= RING)
    for part in range(2):
        @pl.when(on_up)
        def _():
            fw_landed(part)
            send_on(1, own + RING, part).start()

        @pl.when(on_low)
        def _():
            fw_landed(part)
            send_on(0, own - RING, part).start()

    @pl.when(has_low)
    def _():
        to_low.wait_send()
        to_up_like = to_up
        to_up_like.wait_recv()

    @pl.when(has_up)
    def _():
        to_up.wait_send()
        to_low.wait_recv()

    tab_copy = pltpu.make_async_copy(tab_v, tab, load_sem.at[5])
    tab_copy.start()
    tab_copy.wait()

    for copy in sec_copies:
        copy.wait()
    for c in range(CL):
        n = nid[2, c]
        at = (n & (CL - 1)) + jnp.where(n // PER_SECTION > sec, CL, 0)
        square = sec_u[at].astype(F32)
        line = sec_d[pl.ds(at, 1), :]
        head = jnp.where(sq_r >= sq_c, square, 0.0).astype(BF16)
        tail = jnp.where(sq_r < sq_c, square, jnp.where(sq_r == sq_c, line, 0.0)).astype(BF16)
        near, far = zs[2, c, :, pl.ds(0, HALF)], zs[2, c, :, pl.ds(HALF, HALF)]
        coarse[c, :, pl.ds(0, HALF)] = dot_t(near, head)
        coarse[c, :, pl.ds(HALF, HALF)] = dot_t(near, sec_b[at]) + dot(far, tail)

    def finish(group, base, side, part):
        for c in range(part * PER, part * PER + PER):
            at = tab[side, 2, base + c]
            coarse[base + c] = dot_t(zr[group, c], fac[at])

    def take(group, base, side):
        for part in range(PARTS):
            landed(group, part)
        for part in range(PARTS):
            finish(group, base, side, part)

    @pl.when(has_up)
    def _():
        take(0, 8, 1)

    @pl.when(has_low)
    def _():
        take(1, 16, 0)

    @pl.when(own == 1)
    def _():
        take(2, 24, 0)

    @pl.when(own == OWNERS - 2)
    def _():
        take(2, 24, 1)

    for yh in range(4):
        def gather(zz, _):
            m = yh * RING + zz
            acc = coarse[tab[0, 0, m]] + coarse[tab[0, 1, m]]
            acc = acc + coarse[tab[1, 0, m]] + coarse[tab[1, 1, m]]
            acc = acc + coarse[tab[2, 0, m]] + coarse[tab[2, 1, m]]
            total[yh, zz] = acc.astype(BF16)
            return 0

        lax.fori_loop(0, RING, gather, 0)

    def zpiece(d, half=None, part=None):
        rows = pl.ds(0, 32) if half is None else pl.ds(16 * half, 16)
        which = pl.ds(0, 4) if part is None else pl.ds(2 * part, 2)
        return total.at[which, lax.rem(z + d + RING, RING), rows, :]

    def ypiece(d, half=None, part=None):
        to = lax.rem(y + d + RING, RING)
        rows = pl.ds(32, 32) if half is None else pl.ds(32 + 16 * half, 16)
        which = pl.ds(0, 8) if part is None else pl.ds(4 * part, 4)
        return total.at[to // 2, which, rows, pl.ds(pl.multiple_of(lax.rem(to, 2) * HALF, HALF), HALF)]

    axes = ((zpiece, zdev, za3, za4, zad, zas, zat, 2), (ypiece, ydev, ya3, ya4, yad, yas, yat, 4))
    ways = [(a, side, s) for a in range(2) for side, s in ((0, 1), (1, -1))]
    fours, threes, ones, twos = {}, {}, {}, {}
    for half in range(2):
        for a, side, s in ways:
            piece, dev, b3, b4 = axes[a][:4]
            fours[half, a, side] = remote(piece(4 * s, half, side), b4.at[half, side], dev(2 * s))
            fours[half, a, side].start()
        for a, side, s in ways:
            piece, dev, b3, b4 = axes[a][:4]
            threes[half, a, side] = remote(piece(3 * s, half), b3.at[half, side], dev(s))
            threes[half, a, side].start()
    for a, side, s in ways:
        threes[1, a, side].wait_send()
        ones[a, side] = remote(axes[a][0](s), axes[a][4].at[side], axes[a][1](s))
        ones[a, side].start()
    for half in range(2):
        for a, side, s in ways:
            piece, dev, b3, b4, _, bs, bt, n = axes[a]
            fours[half, a, side].wait_recv()
            threes[half, a, side].wait_recv()
            near, far = pl.ds(n * side, n), pl.ds(n * (1 - side), n)
            mine, third, to = piece(2 * s, half), b3.at[half, side], bt.at[half, side]
            to[near] = (mine[near].astype(F32) + third[near].astype(F32) + b4[half, side].astype(F32)).astype(BF16)
            to[far] = (mine[far].astype(F32) + third[far].astype(F32)).astype(BF16)
            twos[half, a, side] = remote(to, bs.at[half, side], dev(2 * s))
            twos[half, a, side].start()
    for copy in list(ones.values()) + list(twos.values()):
        copy.wait_recv()
    sums = []
    for piece, _, _, _, bd, bs, _, _ in axes:
        halves = []
        for half in range(2):
            rows = pl.ds(16 * half, 16)
            acc = piece(0, half)[...].astype(F32)
            for side in range(2):
                acc = acc + bd[side, :, rows, :].astype(F32) + bs[half, side].astype(F32)
            halves.append(acc)
        sums.append(jnp.concatenate(halves, axis=1))
    sum_a, sum_b = sums
    for part in range(2):
        for yh in range(4):
            pa[2 * yh + part] = sum_a[yh, :, part * HALF:(part + 1) * HALF].astype(BF16)
    pb[...] = sum_b.astype(BF16)

    last = []
    for d in (4, 3, 5, 2, 6, 1, 7):
        last.append(remote(pa.at[lax.rem(y + d, RING)], ra.at[d - 1], ydev(d)))
        last.append(remote(pb.at[lax.rem(z + d, RING)], rb.at[d - 1], zdev(d)))
    for copy in last:
        copy.start()
    for copy in last:
        copy.wait_recv()
    done_a, done_b = pa[y].astype(F32), pb[z].astype(F32)
    for d in range(RING - 1):
        done_a = done_a + ra[d].astype(F32)
        done_b = done_b + rb[d].astype(F32)
    out[0, 0, pl.ds(0, 32), :] = done_a.astype(BF16)
    out[0, 0, pl.ds(32, 32), :] = done_b.astype(BF16)
    late = [threes[0, a, side] for a, side, _ in ways]
    for copy in z_sends + list(fours.values()) + late + list(ones.values()) + list(twos.values()) + last:
        copy.wait_send()

    @pl.when(on_up | on_low)
    def _():
        for part in range(2):
            send_on(1, low, part).wait_send()


def on_device(couple, factors, top_reflect, wy_factor, neighbour_ids, kept_rank, merge_map):
    hbm, vmem = (pl.BlockSpec(memory_space=s) for s in (pl.ANY, pltpu.VMEM))
    v = lambda *shape: pltpu.VMEM(shape, BF16)
    return pl.pallas_call(
        kernel,
        name="merge_level",
        out_shape=jax.ShapeDtypeStruct((1, 1, K, HALF), BF16),
        in_specs=[hbm] * 7,
        out_specs=vmem,
        scratch_shapes=[
            pltpu.SMEM((NB, CL), jnp.int32), pltpu.SMEM((CL,), jnp.int32), pltpu.SMEM((NB, CL), jnp.int32),
            v(CL, NB, CW, CW), v(CL, CW, CW), v(CL, K, K), v(CL, K, CW),
            v(CL, HALF, HALF), pltpu.VMEM((CL, HALF), F32), v(2 * CL, HALF, HALF), v(2 * CL, HALF, HALF), pltpu.VMEM((2 * CL, HALF), F32),
            v(NB, CL, K, CW), v(3, CL, K, CW), v(2 * PER, K, CW),
            pltpu.VMEM((2, 8, 128), jnp.int32), pltpu.VMEM((3, 8, 128), jnp.int32), pltpu.SMEM((3, 8, 128), jnp.int32),
            pltpu.VMEM((EMPTY + 1, K, CW), F32), v(4, RING, K, CW),
            v(2, 2, 4, 16, CW), v(2, 2, 2, 16, CW), v(2, 4, 32, CW), v(2, 2, 4, 16, CW), v(2, 2, 4, 16, CW),
            v(2, 2, 8, 16, HALF), v(2, 2, 4, 16, HALF), v(2, 8, 32, HALF), v(2, 2, 8, 16, HALF), v(2, 2, 8, 16, HALF),
            v(8, 32, HALF), v(8, 32, HALF), v(7, 32, HALF), v(7, 32, HALF),
            pltpu.SemaphoreType.DMA((13,)), pltpu.SemaphoreType.DMA((SEMS,)), pltpu.SemaphoreType.DMA((SEMS,)),
        ],
        compiler_params=pltpu.CompilerParams(collective_id=0, has_side_effects=True, vmem_limit_bytes=62 << 20),
    )(couple, factors, top_reflect, wy_factor.transpose(0, 2, 1), neighbour_ids.T, kept_rank, merge_map.T)


def solution(mesh):
    own = ("sec", "own", "tile")
    in_specs = (P(own, None, None, None), P(own, None, None), P(own, None, None), P(own, None, None),
                P(own, None), P(own), P(own, None))
    return jax.shard_map(on_device, mesh=mesh, in_specs=in_specs, out_specs=P("sec", "own", None, "tile"), check_vma=False)
```

```python
import jax
import jax.numpy as jnp
from jax import lax
from jax.experimental import pallas as pl
from jax.experimental.pallas import tpu as pltpu
from jax.sharding import PartitionSpec as P

MESH = pl.DeviceIdType.MESH
F32 = jnp.float32
BF16 = jnp.bfloat16
CL, NB, CW, K = 8, 3, 256, 64
HALF = CW // 2
RING = 8
OWNERS = 32
SECTIONS = 8
PER_SECTION = 512
PARTS = 4
PER = CL // PARTS
SEMS = 72
EMPTY = 32


def dot(a, b):
    return lax.dot_general(a, b, (((1,), (0,)), ((), ())), preferred_element_type=F32)


def dot_t(a, b):
    return lax.dot_general(a, b, (((1,), (1,)), ((), ())), preferred_element_type=F32)


def kernel(couple, factors, reflect, wy, nid_h, rank_h, mmap_h, out,
           nid, rank, mmap, couple_v, fac, refl_v, wy_v, pack, diag, sec_b, sec_u, sec_d, zs, zr, fw, tab_s, tab_v, tab, coarse, part_total, total,
           za3, za4, zad, zas, zat, ya3, ya4, yad, yas, yat, pa, pb, ra, rb,
           load_sem, ss, rs):
    sec, own, tile = lax.axis_index("sec"), lax.axis_index("own"), lax.axis_index("tile")
    z, y = lax.rem(own, RING), (own // RING) * 2 + tile

    def zdev(d):
        return {"own": (own // RING) * RING + lax.rem(z + d + RING, RING)}

    def ydev(d):
        to = lax.rem(y + d + RING, RING)
        return {"own": (to // 2) * RING + z, "tile": lax.rem(to, 2)}

    def sdev(d):
        return {"sec": lax.rem(sec + d + SECTIONS, SECTIONS)}

    has_low, has_up = own > 0, own < OWNERS - 1
    low = jnp.where(has_low, own - 1, own + 1)
    up = jnp.where(has_up, own + 1, own - 1)

    ints = [pltpu.make_async_copy(a, b, load_sem.at[6 + i]) for i, (a, b) in enumerate(((mmap_h, mmap), (nid_h, nid), (rank_h, rank)))]
    loads = [pltpu.make_async_copy(factors, fac, load_sem.at[0]),
             pltpu.make_async_copy(wy, wy_v, load_sem.at[1]),
             pltpu.make_async_copy(reflect, refl_v, load_sem.at[2])]
    couples = []
    for part in range(PARTS):
        at = pl.ds(part * PER, PER)
        couples.append(pltpu.make_async_copy(couple.at[at], couple_v.at[at], load_sem.at[9 + part]))
    for copy in ints + loads + couples:
        copy.start()

    barrier = pltpu.get_barrier_semaphore()

    def greet(to):
        pl.semaphore_signal(barrier, inc=1, device_id=to, device_id_type=MESH)

    greet(sdev(1))
    greet(sdev(-1))

    @pl.when(has_low)
    def _():
        greet({"own": own - 1})

    @pl.when(has_up)
    def _():
        greet({"own": own + 1})

    for d in (2, -2, 1, -1):
        greet(zdev(d))
        greet(ydev(d))

    at_end = own == OWNERS - 1
    relay = ((own == 22) & (tile == 1)) | ((own == 6) & (tile == 0))
    relay_dev = {"own": jnp.where(tile == 0, 22, 6), "tile": 1 - tile}

    @pl.when(at_end)
    def _():
        greet(relay_dev)

    @pl.when(relay)
    def _():
        greet({"own": OWNERS - 1, "tile": 1 - tile})

    met = 2 + 8 + has_low.astype(jnp.int32) + has_up.astype(jnp.int32) + (at_end | relay).astype(jnp.int32)
    early = z < RING // 2
    late = z >= RING // 2

    count = [0]

    def remote(src, dst, to):
        i = count[0]
        count[0] += 1
        return pltpu.make_async_remote_copy(src_ref=src, dst_ref=dst, send_sem=ss.at[i], recv_sem=rs.at[i],
                                            device_id=to, device_id_type=MESH)

    blocks, squares = [], []
    for side, d in ((0, 1), (1, -1)):
        at = pl.ds(side * CL, CL)
        blocks.append(remote(fac.at[:, pl.ds(HALF, HALF), pl.ds(0, HALF)], sec_b.at[at], sdev(d)))
        squares += [remote(pack, sec_u.at[at], sdev(d)), remote(diag, sec_d.at[at], sdev(d))]
    sec_copies = blocks + squares
    sq_r = lax.broadcasted_iota(jnp.int32, (HALF, HALF), 0)
    sq_c = lax.broadcasted_iota(jnp.int32, (HALF, HALF), 1)

    def open_up():
        pl.semaphore_wait(barrier, met)
        for copy in blocks:
            copy.start()

    def pack_up():
        for c in range(CL):
            lower = fac[c, pl.ds(HALF, HALF), pl.ds(HALF, HALF)].astype(F32)
            diag[pl.ds(c, 1), :] = jnp.sum(jnp.where(sq_r == sq_c, lower, 0.0), axis=0, keepdims=True)
            upper = fac[c, pl.ds(0, HALF), pl.ds(0, HALF)].astype(F32)
            pack[c] = jnp.where(sq_r >= sq_c, upper, lower.T).astype(BF16)

    base_sem = count[0]
    count[0] += 3 * PARTS
    fw_sem = count[0]
    count[0] += 2
    on_sem = count[0]
    count[0] += 2
    for copy in loads + ints:
        copy.wait()
    r_iota = lax.broadcasted_iota(jnp.int32, (K, CW), 0)
    c_iota = lax.broadcasted_iota(jnp.int32, (K, CW), 1)
    eye = jnp.where(r_iota == c_iota, 1.0, 0.0)
    low_group = jnp.where(has_low, 0, 2)
    up_group = jnp.where(has_up, 1, 2)
    cross_low = (z == 0) & has_low
    cross_up = (z == RING - 1) & has_up
    tops = []
    for c in range(CL):
        t = eye - dot(refl_v[c], wy_v[c])
        t = jnp.where(r_iota < rank[c], t, 0.0).astype(BF16)
        tops.append(dot(t, fac[c]).astype(BF16))
    plain, by_way, by_relay = {}, {}, {}
    for part in range(PARTS):
        at = pl.ds(part * PER, PER)
        for j in range(2):
            group = (low_group, up_group)[j]
            plain[j, part] = pltpu.make_async_remote_copy(
                src_ref=zs.at[j, at], dst_ref=zr.at[group, at], send_sem=ss.at[base_sem + j * PARTS + part],
                recv_sem=rs.at[base_sem + group * PARTS + part], device_id={"own": (low, up)[j]}, device_id_type=MESH)
            if part < 2:
                by_way[j, part] = pltpu.make_async_remote_copy(
                    src_ref=zs.at[j, at], dst_ref=fw.at[at], send_sem=ss.at[base_sem + j * PARTS + part],
                    recv_sem=rs.at[fw_sem + part], device_id=zdev((-1, 1)[j]), device_id_type=MESH)
        if part < 2:
            by_relay[part] = pltpu.make_async_remote_copy(
                src_ref=zs.at[1, at], dst_ref=fw.at[at], send_sem=ss.at[base_sem + PARTS + part],
                recv_sem=rs.at[fw_sem + part], device_id=relay_dev, device_id_type=MESH)

    def z_send(part):
        for j in (1, 0):
            if part >= 2:
                plain[j, part].start()
                continue
            crossing = (cross_low, cross_up)[j]

            @pl.when(crossing)
            def _():
                by_way[j, part].start()

            if j == 1:
                @pl.when(at_end)
                def _():
                    by_relay[part].start()

                crossing = crossing | at_end

            @pl.when(jnp.logical_not(crossing))
            def _():
                plain[j, part].start()

    @pl.when(early)
    def _():
        pack_up()

    for part in range(PARTS):
        couples[part].wait()
        for j in (1, 0, 2):
            for c in range(part * PER, part * PER + PER):
                zs[j, c] = dot(tops[c], couple_v[c, j]).astype(BF16)

        @pl.when(late)
        def _():
            if part == 0:
                open_up()
            z_send(part)

    @pl.when(early)
    def _():
        open_up()
        for part in range(PARTS):
            z_send(part)

    @pl.when(late)
    def _():
        pack_up()

    for copy in squares:
        copy.start()

    lane = lax.broadcasted_iota(jnp.int32, (8, 128), 1)
    row = lax.broadcasted_iota(jnp.int32, (8, 128), 0)

    def table(groups):
        first = jnp.full((8, 128), EMPTY, jnp.int32)
        second = jnp.full((8, 128), EMPTY, jnp.int32)
        local = jnp.zeros((8, 128), jnp.int32)
        for j, base, wanted in groups:
            for c in range(CL):
                hit = lane == mmap[j, c]
                if wanted is not None:
                    hit = hit & wanted
                second = jnp.where(hit & (first != EMPTY), base + c, second)
                first = jnp.where(hit & (first == EMPTY), base + c, first)
                local = jnp.where(lane == base + c, nid[j, c] & (CL - 1), local)
        return jnp.where(row == 0, first, jnp.where(row == 1, second, local))

    at_low_end = jnp.full((8, 128), own, jnp.int32) == 0
    at_up_end = jnp.full((8, 128), own, jnp.int32) == OWNERS - 1
    tab_s[0] = table([(0, 8, None), (1, 24, at_up_end)])
    tab_s[1] = table([(1, 16, None), (0, 24, at_low_end)])
    tab_v[2] = table([(2, 0, None)])
    nothing = jnp.where(row < 2, EMPTY, 0)

    @pl.when(jnp.logical_not(has_low))
    def _():
        tab_v[0] = nothing

    @pl.when(jnp.logical_not(has_up))
    def _():
        tab_v[1] = nothing

    coarse[EMPTY] = jnp.zeros((K, CW), F32)
    to_low = remote(tab_s.at[0], tab_v.at[1], {"own": low})
    to_up = remote(tab_s.at[1], tab_v.at[0], {"own": up})

    @pl.when(has_low)
    def _():
        to_low.start()

    @pl.when(has_up)
    def _():
        to_up.start()

    def send_on(group, to, part):
        at = pl.ds(part * PER, PER)
        return pltpu.make_async_remote_copy(
            src_ref=fw.at[at], dst_ref=zr.at[group, at], send_sem=ss.at[on_sem + part],
            recv_sem=rs.at[base_sem + group * PARTS + part], device_id={"own": to}, device_id_type=MESH)

    def fw_landed(part):
        at = pl.ds(part * PER, PER)
        pltpu.make_async_remote_copy(src_ref=zs.at[0, at], dst_ref=fw.at[at], send_sem=ss.at[base_sem], recv_sem=rs.at[fw_sem + part],
                                     device_id=zdev(1), device_id_type=MESH).wait_recv()

    def landed(group, part):
        at = pl.ds(part * PER, PER)
        pltpu.make_async_remote_copy(
            src_ref=zs.at[0, at], dst_ref=zr.at[group, at], send_sem=ss.at[base_sem], recv_sem=rs.at[base_sem + group * PARTS + part],
            device_id={"own": low}, device_id_type=MESH).wait_recv()

    on_up = (z == 0) & (own < OWNERS - RING)
    on_low = (z == RING - 1) & (own >= RING)
    for part in range(2):
        @pl.when(on_up)
        def _():
            fw_landed(part)
            send_on(1, own + RING, part).start()

        @pl.when(on_low)
        def _():
            fw_landed(part)
            send_on(0, own - RING, part).start()

        @pl.when(relay)
        def _():
            fw_landed(part)
            pltpu.make_async_remote_copy(
                src_ref=fw.at[pl.ds(part * PER, PER)], dst_ref=zr.at[2, pl.ds(part * PER, PER)], send_sem=ss.at[on_sem + part],
                recv_sem=rs.at[base_sem + 2 * PARTS + part], device_id={"own": OWNERS - 2, "tile": 1 - tile}, device_id_type=MESH).start()

    @pl.when(has_low)
    def _():
        to_low.wait_send()
        to_up_like = to_up
        to_up_like.wait_recv()

    @pl.when(has_up)
    def _():
        to_up.wait_send()
        to_low.wait_recv()

    tab_copy = pltpu.make_async_copy(tab_v, tab, load_sem.at[5])
    tab_copy.start()
    tab_copy.wait()

    for copy in sec_copies:
        copy.wait()
    for c in range(CL):
        n = nid[2, c]
        at = (n & (CL - 1)) + jnp.where(n // PER_SECTION > sec, CL, 0)
        square = sec_u[at].astype(F32)
        line = sec_d[pl.ds(at, 1), :]
        head = jnp.where(sq_r >= sq_c, square, 0.0).astype(BF16)
        tail = jnp.where(sq_r < sq_c, square, jnp.where(sq_r == sq_c, line, 0.0)).astype(BF16)
        near, far = zs[2, c, :, pl.ds(0, HALF)], zs[2, c, :, pl.ds(HALF, HALF)]
        coarse[c, :, pl.ds(0, HALF)] = dot_t(near, head)
        coarse[c, :, pl.ds(HALF, HALF)] = dot_t(near, sec_b[at]) + dot(far, tail)

    def finish(group, base, side, part):
        for c in range(part * PER, part * PER + PER):
            at = tab[side, 2, base + c]
            coarse[base + c] = dot_t(zr[group, c], fac[at])

    def take(group, base, side):
        for part in range(PARTS):
            landed(group, part)
            finish(group, base, side, part)

    up_last = z >= RING - 2
    side_first = jnp.where(up_last, 0, 1)
    side_last = 1 - side_first

    @pl.when(jnp.logical_not(up_last))
    def _():
        take(0, 8, 1)

    @pl.when(up_last)
    def _():
        take(1, 16, 0)

    for yh in range(4):
        def gather(zz, _):
            m = yh * RING + zz
            acc = coarse[tab[2, 0, m]] + coarse[tab[2, 1, m]]
            part_total[yh, zz] = acc + coarse[tab[side_first, 0, m]] + coarse[tab[side_first, 1, m]]
            return 0

        lax.fori_loop(0, RING, gather, 0)

    @pl.when(jnp.logical_not(up_last) & has_low)
    def _():
        take(1, 16, 0)

    @pl.when(up_last & has_up)
    def _():
        take(0, 8, 1)

    @pl.when(own == 1)
    def _():
        take(2, 24, 0)

    @pl.when(own == OWNERS - 2)
    def _():
        take(2, 24, 1)

    for yh in range(4):
        def gather_last(zz, _):
            m = yh * RING + zz
            acc = part_total[yh, zz] + coarse[tab[side_last, 0, m]] + coarse[tab[side_last, 1, m]]
            total[yh, zz] = acc.astype(BF16)
            return 0

        lax.fori_loop(0, RING, gather_last, 0)

    def zpiece(d, half=None, part=None):
        rows = pl.ds(0, 32) if half is None else pl.ds(16 * half, 16)
        which = pl.ds(0, 4) if part is None else pl.ds(2 * part, 2)
        return total.at[which, lax.rem(z + d + RING, RING), rows, :]

    def ypiece(d, half=None, part=None):
        to = lax.rem(y + d + RING, RING)
        rows = pl.ds(32, 32) if half is None else pl.ds(32 + 16 * half, 16)
        which = pl.ds(0, 8) if part is None else pl.ds(4 * part, 4)
        return total.at[to // 2, which, rows, pl.ds(pl.multiple_of(lax.rem(to, 2) * HALF, HALF), HALF)]

    axes = ((zpiece, zdev, za3, za4, zad, zas, zat, 2), (ypiece, ydev, ya3, ya4, yad, yas, yat, 4))
    ways = [(a, side, s) for a in range(2) for side, s in ((0, 1), (1, -1))]
    fours, threes, ones, twos = {}, {}, {}, {}
    for half in range(2):
        for a, side, s in ways:
            piece, dev, b3, b4 = axes[a][:4]
            fours[half, a, side] = remote(piece(4 * s, half, side), b4.at[half, side], dev(2 * s))
            fours[half, a, side].start()
        for a, side, s in ways:
            piece, dev, b3, b4 = axes[a][:4]
            threes[half, a, side] = remote(piece(3 * s, half), b3.at[half, side], dev(s))
            threes[half, a, side].start()
    for a, side, s in ways:
        threes[1, a, side].wait_send()
        ones[a, side] = remote(axes[a][0](s), axes[a][4].at[side], axes[a][1](s))
        ones[a, side].start()
    for half in range(2):
        for a, side, s in ways:
            piece, dev, b3, b4, _, bs, bt, n = axes[a]
            fours[half, a, side].wait_recv()
            threes[half, a, side].wait_recv()
            near, far = pl.ds(n * side, n), pl.ds(n * (1 - side), n)
            mine, third, to = piece(2 * s, half), b3.at[half, side], bt.at[half, side]
            to[near] = (mine[near].astype(F32) + third[near].astype(F32) + b4[half, side].astype(F32)).astype(BF16)
            to[far] = (mine[far].astype(F32) + third[far].astype(F32)).astype(BF16)
            twos[half, a, side] = remote(to, bs.at[half, side], dev(2 * s))
            twos[half, a, side].start()
    last = []
    for a in (1, 0):
        piece, _, _, _, bd, bs, _, _ = axes[a]
        for side in range(2):
            ones[a, side].wait_recv()
            for half in range(2):
                twos[half, a, side].wait_recv()
        halves = []
        for half in range(2):
            rows = pl.ds(16 * half, 16)
            acc = piece(0, half)[...].astype(F32)
            for side in range(2):
                acc = acc + bd[side, :, rows, :].astype(F32) + bs[half, side].astype(F32)
            halves.append(acc)
        done = jnp.concatenate(halves, axis=1).astype(BF16)
        if a == 1:
            pb[...] = done
        else:
            for part in range(2):
                for yh in range(4):
                    pa[2 * yh + part] = done[yh, :, part * HALF:(part + 1) * HALF]
        for d in (4, 3, 5, 2, 6, 1, 7):
            if a == 1:
                copy = remote(pb.at[lax.rem(z + d, RING)], rb.at[d - 1], zdev(d))
            else:
                copy = remote(pa.at[lax.rem(y + d, RING)], ra.at[d - 1], ydev(d))
            copy.start()
            last.append(copy)
    for copy in last:
        copy.wait_recv()
    done_a, done_b = pa[y].astype(F32), pb[z].astype(F32)
    for d in range(RING - 1):
        done_a = done_a + ra[d].astype(F32)
        done_b = done_b + rb[d].astype(F32)
    out[0, 0, pl.ds(0, 32), :] = done_a.astype(BF16)
    out[0, 0, pl.ds(32, 32), :] = done_b.astype(BF16)
    late = [threes[0, a, side] for a, side, _ in ways]
    for copy in list(plain.values()) + list(fours.values()) + late + list(ones.values()) + list(twos.values()) + last:
        copy.wait_send()

    @pl.when(on_up | on_low | relay)
    def _():
        for part in range(2):
            send_on(1, low, part).wait_send()


def on_device(couple, factors, top_reflect, wy_factor, neighbour_ids, kept_rank, merge_map):
    hbm, vmem = (pl.BlockSpec(memory_space=s) for s in (pl.ANY, pltpu.VMEM))
    v = lambda *shape: pltpu.VMEM(shape, BF16)
    return pl.pallas_call(
        kernel,
        name="merge_level",
        out_shape=jax.ShapeDtypeStruct((1, 1, K, HALF), BF16),
        in_specs=[hbm] * 7,
        out_specs=vmem,
        scratch_shapes=[
            pltpu.SMEM((NB, CL), jnp.int32), pltpu.SMEM((CL,), jnp.int32), pltpu.SMEM((NB, CL), jnp.int32),
            v(CL, NB, CW, CW), v(CL, CW, CW), v(CL, K, K), v(CL, K, CW),
            v(CL, HALF, HALF), pltpu.VMEM((CL, HALF), F32), v(2 * CL, HALF, HALF), v(2 * CL, HALF, HALF), pltpu.VMEM((2 * CL, HALF), F32),
            v(NB, CL, K, CW), v(3, CL, K, CW), v(2 * PER, K, CW),
            pltpu.VMEM((2, 8, 128), jnp.int32), pltpu.VMEM((3, 8, 128), jnp.int32), pltpu.SMEM((3, 8, 128), jnp.int32),
            pltpu.VMEM((EMPTY + 1, K, CW), F32), pltpu.VMEM((4, RING, K, CW), F32), v(4, RING, K, CW),
            v(2, 2, 4, 16, CW), v(2, 2, 2, 16, CW), v(2, 4, 32, CW), v(2, 2, 4, 16, CW), v(2, 2, 4, 16, CW),
            v(2, 2, 8, 16, HALF), v(2, 2, 4, 16, HALF), v(2, 8, 32, HALF), v(2, 2, 8, 16, HALF), v(2, 2, 8, 16, HALF),
            v(8, 32, HALF), v(8, 32, HALF), v(7, 32, HALF), v(7, 32, HALF),
            pltpu.SemaphoreType.DMA((13,)), pltpu.SemaphoreType.DMA((SEMS,)), pltpu.SemaphoreType.DMA((SEMS,)),
        ],
        compiler_params=pltpu.CompilerParams(collective_id=0, has_side_effects=True, vmem_limit_bytes=62 << 20),
    )(couple, factors, top_reflect, wy_factor.transpose(0, 2, 1), neighbour_ids.T, kept_rank, merge_map.T)


def solution(mesh):
    own = ("sec", "own", "tile")
    in_specs = (P(own, None, None, None), P(own, None, None), P(own, None, None), P(own, None, None),
                P(own, None), P(own), P(own, None))
    return jax.shard_map(on_device, mesh=mesh, in_specs=in_specs, out_specs=P("sec", "own", None, "tile"), check_vma=False)
```

```python
import jax
import jax.numpy as jnp
from jax import lax
from jax.experimental import pallas as pl
from jax.experimental.pallas import tpu as pltpu
from jax.sharding import PartitionSpec as P

MESH = pl.DeviceIdType.MESH
F32 = jnp.float32
BF16 = jnp.bfloat16
CL, NB, CW, K = 8, 3, 256, 64
HALF = CW // 2
RING = 8
OWNERS = 32
SECTIONS = 8
PER_SECTION = 512
PARTS = 4
PER = CL // PARTS
SEMS = 72
EMPTY = 32


def dot(a, b):
    return lax.dot_general(a, b, (((1,), (0,)), ((), ())), preferred_element_type=F32)


def dot_t(a, b):
    return lax.dot_general(a, b, (((1,), (1,)), ((), ())), preferred_element_type=F32)


def kernel(couple, factors, reflect, wy, nid_h, rank_h, mmap_h, out,
           nid, rank, mmap, couple_v, fac, refl_v, wy_v, pack, diag, sec_b, sec_u, sec_d, zs, zr, fw, tab_s, tab_v, tab, coarse, part_total, total,
           za3, za4, zad, zas, zat, ya3, ya4, yad, yas, yat, pa, pb, ra, rb,
           load_sem, ss, rs):
    sec, own, tile = lax.axis_index("sec"), lax.axis_index("own"), lax.axis_index("tile")
    z, y = lax.rem(own, RING), (own // RING) * 2 + tile

    def zdev(d):
        return {"own": (own // RING) * RING + lax.rem(z + d + RING, RING)}

    def ydev(d):
        to = lax.rem(y + d + RING, RING)
        return {"own": (to // 2) * RING + z, "tile": lax.rem(to, 2)}

    def sdev(d):
        return {"sec": lax.rem(sec + d + SECTIONS, SECTIONS)}

    has_low, has_up = own > 0, own < OWNERS - 1
    low = jnp.where(has_low, own - 1, own + 1)
    up = jnp.where(has_up, own + 1, own - 1)

    ints = [pltpu.make_async_copy(a, b, load_sem.at[6 + i]) for i, (a, b) in enumerate(((mmap_h, mmap), (nid_h, nid), (rank_h, rank)))]
    loads = [pltpu.make_async_copy(factors, fac, load_sem.at[0]),
             pltpu.make_async_copy(wy, wy_v, load_sem.at[1]),
             pltpu.make_async_copy(reflect, refl_v, load_sem.at[2])]
    couples = []
    for part in range(PARTS):
        at = pl.ds(part * PER, PER)
        couples.append(pltpu.make_async_copy(couple.at[at], couple_v.at[at], load_sem.at[9 + part]))
    for copy in ints + loads + couples:
        copy.start()

    barrier = pltpu.get_barrier_semaphore()

    def greet(to):
        pl.semaphore_signal(barrier, inc=1, device_id=to, device_id_type=MESH)

    greet(sdev(1))
    greet(sdev(-1))

    @pl.when(has_low)
    def _():
        greet({"own": own - 1})

    @pl.when(has_up)
    def _():
        greet({"own": own + 1})

    for d in (2, -2, 1, -1):
        greet(zdev(d))
        greet(ydev(d))

    at_start = own == 0
    at_end = own == OWNERS - 1
    for_start = ((own == 25) & (tile == 1)) | ((own == 9) & (tile == 0))
    relay = ((own == 22) & (tile == 1)) | ((own == 6) & (tile == 0)) | for_start
    relay_dev = {"own": jnp.where(at_start, jnp.where(tile == 0, 25, 9), jnp.where(tile == 0, 22, 6)), "tile": 1 - tile}
    relay_from = jnp.where(for_start, 0, OWNERS - 1)
    relay_to = jnp.where(for_start, 1, OWNERS - 2)

    @pl.when(at_start | at_end)
    def _():
        greet(relay_dev)

    @pl.when(relay)
    def _():
        greet({"own": relay_from, "tile": 1 - tile})

    met = 2 + 8 + has_low.astype(jnp.int32) + has_up.astype(jnp.int32) + (at_start | at_end | relay).astype(jnp.int32)
    early = z < RING // 2
    late = z >= RING // 2

    count = [0]

    def remote(src, dst, to):
        i = count[0]
        count[0] += 1
        return pltpu.make_async_remote_copy(src_ref=src, dst_ref=dst, send_sem=ss.at[i], recv_sem=rs.at[i],
                                            device_id=to, device_id_type=MESH)

    blocks, squares = [], []
    for side, d in ((0, 1), (1, -1)):
        at = pl.ds(side * CL, CL)
        blocks.append(remote(fac.at[:, pl.ds(HALF, HALF), pl.ds(0, HALF)], sec_b.at[at], sdev(d)))
        squares += [remote(pack, sec_u.at[at], sdev(d)), remote(diag, sec_d.at[at], sdev(d))]
    sec_copies = blocks + squares
    sq_r = lax.broadcasted_iota(jnp.int32, (HALF, HALF), 0)
    sq_c = lax.broadcasted_iota(jnp.int32, (HALF, HALF), 1)

    def open_up():
        pl.semaphore_wait(barrier, met)
        for copy in blocks:
            copy.start()

    def pack_up():
        for c in range(CL):
            lower = fac[c, pl.ds(HALF, HALF), pl.ds(HALF, HALF)].astype(F32)
            diag[pl.ds(c, 1), :] = jnp.sum(jnp.where(sq_r == sq_c, lower, 0.0), axis=0, keepdims=True)
            upper = fac[c, pl.ds(0, HALF), pl.ds(0, HALF)].astype(F32)
            pack[c] = jnp.where(sq_r >= sq_c, upper, lower.T).astype(BF16)

    base_sem = count[0]
    count[0] += 3 * PARTS
    fw_sem = count[0]
    count[0] += 2
    on_sem = count[0]
    count[0] += 2
    for copy in loads + ints:
        copy.wait()
    r_iota = lax.broadcasted_iota(jnp.int32, (K, CW), 0)
    c_iota = lax.broadcasted_iota(jnp.int32, (K, CW), 1)
    eye = jnp.where(r_iota == c_iota, 1.0, 0.0)
    low_group = jnp.where(has_low, 0, 2)
    up_group = jnp.where(has_up, 1, 2)
    cross_low = (z == 0) & has_low
    cross_up = (z == RING - 1) & has_up
    tops = []
    for c in range(CL):
        t = eye - dot(refl_v[c], wy_v[c])
        t = jnp.where(r_iota < rank[c], t, 0.0).astype(BF16)
        tops.append(dot(t, fac[c]).astype(BF16))
    plain, by_way, by_relay = {}, {}, {}
    for part in range(PARTS):
        at = pl.ds(part * PER, PER)
        for j in range(2):
            group = (low_group, up_group)[j]
            plain[j, part] = pltpu.make_async_remote_copy(
                src_ref=zs.at[j, at], dst_ref=zr.at[group, at], send_sem=ss.at[base_sem + j * PARTS + part],
                recv_sem=rs.at[base_sem + group * PARTS + part], device_id={"own": (low, up)[j]}, device_id_type=MESH)
            if part < 2:
                by_way[j, part] = pltpu.make_async_remote_copy(
                    src_ref=zs.at[j, at], dst_ref=fw.at[at], send_sem=ss.at[base_sem + j * PARTS + part],
                    recv_sem=rs.at[fw_sem + part], device_id=zdev((-1, 1)[j]), device_id_type=MESH)
                by_relay[j, part] = pltpu.make_async_remote_copy(
                    src_ref=zs.at[j, at], dst_ref=fw.at[at], send_sem=ss.at[base_sem + j * PARTS + part],
                    recv_sem=rs.at[fw_sem + part], device_id=relay_dev, device_id_type=MESH)

    def z_send(part):
        for j in (1, 0):
            if part >= 2:
                plain[j, part].start()
                continue
            crossing = (cross_low, cross_up)[j]

            @pl.when(crossing)
            def _():
                by_way[j, part].start()

            doubled = (at_start, at_end)[j]

            @pl.when(doubled)
            def _():
                by_relay[j, part].start()

            crossing = crossing | doubled

            @pl.when(jnp.logical_not(crossing))
            def _():
                plain[j, part].start()

    lane = lax.broadcasted_iota(jnp.int32, (8, 128), 1)
    row = lax.broadcasted_iota(jnp.int32, (8, 128), 0)

    def table(groups):
        first = jnp.full((8, 128), EMPTY, jnp.int32)
        second = jnp.full((8, 128), EMPTY, jnp.int32)
        local = jnp.zeros((8, 128), jnp.int32)
        for j, base, wanted in groups:
            for c in range(CL):
                hit = lane == mmap[j, c]
                if wanted is not None:
                    hit = hit & wanted
                second = jnp.where(hit & (first != EMPTY), base + c, second)
                first = jnp.where(hit & (first == EMPTY), base + c, first)
                local = jnp.where(lane == base + c, nid[j, c] & (CL - 1), local)
        return jnp.where(row == 0, first, jnp.where(row == 1, second, local))

    at_low_end = jnp.full((8, 128), own, jnp.int32) == 0
    at_up_end = jnp.full((8, 128), own, jnp.int32) == OWNERS - 1
    to_low = remote(tab_s.at[0], tab_v.at[1], {"own": low})
    to_up = remote(tab_s.at[1], tab_v.at[0], {"own": up})

    def fill_tables():
        tab_s[0] = table([(0, 8, None), (1, 24, at_up_end)])
        tab_s[1] = table([(1, 16, None), (0, 24, at_low_end)])
        tab_v[2] = table([(2, 0, None)])
        nothing = jnp.where(row < 2, EMPTY, 0)

        @pl.when(jnp.logical_not(has_low))
        def _():
            tab_v[0] = nothing

        @pl.when(jnp.logical_not(has_up))
        def _():
            tab_v[1] = nothing

        coarse[EMPTY] = jnp.zeros((K, CW), F32)

    def send_tables():
        @pl.when(has_low)
        def _():
            to_low.start()

        @pl.when(has_up)
        def _():
            to_up.start()

    @pl.when(early)
    def _():
        fill_tables()
        pack_up()

    for part in range(PARTS):
        couples[part].wait()
        for j in (1, 0, 2):
            for c in range(part * PER, part * PER + PER):
                zs[j, c] = dot(tops[c], couple_v[c, j]).astype(BF16)

        @pl.when(late)
        def _():
            if part == 0:
                open_up()
            z_send(part)

    @pl.when(early)
    def _():
        open_up()
        for part in range(PARTS):
            z_send(part)
        send_tables()

    @pl.when(late)
    def _():
        fill_tables()
        send_tables()
        pack_up()

    for copy in squares:
        copy.start()

    def send_on(group, to, part):
        at = pl.ds(part * PER, PER)
        return pltpu.make_async_remote_copy(
            src_ref=fw.at[at], dst_ref=zr.at[group, at], send_sem=ss.at[on_sem + part],
            recv_sem=rs.at[base_sem + group * PARTS + part], device_id={"own": to}, device_id_type=MESH)

    def fw_landed(part):
        at = pl.ds(part * PER, PER)
        pltpu.make_async_remote_copy(src_ref=zs.at[0, at], dst_ref=fw.at[at], send_sem=ss.at[base_sem], recv_sem=rs.at[fw_sem + part],
                                     device_id=zdev(1), device_id_type=MESH).wait_recv()

    def landed(group, part):
        at = pl.ds(part * PER, PER)
        pltpu.make_async_remote_copy(
            src_ref=zs.at[0, at], dst_ref=zr.at[group, at], send_sem=ss.at[base_sem], recv_sem=rs.at[base_sem + group * PARTS + part],
            device_id={"own": low}, device_id_type=MESH).wait_recv()

    on_up = (z == 0) & (own < OWNERS - RING)
    on_low = (z == RING - 1) & (own >= RING)
    for part in range(2):
        @pl.when(on_up)
        def _():
            fw_landed(part)
            send_on(1, own + RING, part).start()

        @pl.when(on_low)
        def _():
            fw_landed(part)
            send_on(0, own - RING, part).start()

        @pl.when(relay)
        def _():
            fw_landed(part)
            pltpu.make_async_remote_copy(
                src_ref=fw.at[pl.ds(part * PER, PER)], dst_ref=zr.at[2, pl.ds(part * PER, PER)], send_sem=ss.at[on_sem + part],
                recv_sem=rs.at[base_sem + 2 * PARTS + part], device_id={"own": relay_to, "tile": 1 - tile}, device_id_type=MESH).start()

    @pl.when(has_low)
    def _():
        to_low.wait_send()
        to_up_like = to_up
        to_up_like.wait_recv()

    @pl.when(has_up)
    def _():
        to_up.wait_send()
        to_low.wait_recv()

    tab_copy = pltpu.make_async_copy(tab_v, tab, load_sem.at[5])
    tab_copy.start()
    tab_copy.wait()

    for copy in sec_copies:
        copy.wait()
    for c in range(CL):
        n = nid[2, c]
        at = (n & (CL - 1)) + jnp.where(n // PER_SECTION > sec, CL, 0)
        square = sec_u[at].astype(F32)
        line = sec_d[pl.ds(at, 1), :]
        head = jnp.where(sq_r >= sq_c, square, 0.0).astype(BF16)
        tail = jnp.where(sq_r < sq_c, square, jnp.where(sq_r == sq_c, line, 0.0)).astype(BF16)
        near, far = zs[2, c, :, pl.ds(0, HALF)], zs[2, c, :, pl.ds(HALF, HALF)]
        coarse[c, :, pl.ds(0, HALF)] = dot_t(near, head)
        coarse[c, :, pl.ds(HALF, HALF)] = dot_t(near, sec_b[at]) + dot(far, tail)

    def finish(group, base, side, part):
        for c in range(part * PER, part * PER + PER):
            at = tab[side, 2, base + c]
            coarse[base + c] = dot_t(zr[group, c], fac[at])

    def take(group, base, side):
        for part in range(PARTS):
            landed(group, part)
        for part in range(PARTS):
            finish(group, base, side, part)

    up_last = z >= RING - 2
    side_first = jnp.where(up_last, 0, 1)
    side_last = 1 - side_first

    @pl.when(jnp.logical_not(up_last))
    def _():
        take(0, 8, 1)

    @pl.when(up_last)
    def _():
        take(1, 16, 0)

    for yh in range(4):
        def gather(zz, _):
            m = yh * RING + zz
            acc = coarse[tab[2, 0, m]] + coarse[tab[2, 1, m]]
            part_total[yh, zz] = acc + coarse[tab[side_first, 0, m]] + coarse[tab[side_first, 1, m]]
            return 0

        lax.fori_loop(0, RING, gather, 0)

    @pl.when(jnp.logical_not(up_last) & has_low)
    def _():
        take(1, 16, 0)

    @pl.when(up_last & has_up)
    def _():
        take(0, 8, 1)

    @pl.when(own == 1)
    def _():
        take(2, 24, 0)

    @pl.when(own == OWNERS - 2)
    def _():
        take(2, 24, 1)

    for yh in range(4):
        def gather_last(zz, _):
            m = yh * RING + zz
            acc = part_total[yh, zz] + coarse[tab[side_last, 0, m]] + coarse[tab[side_last, 1, m]]
            total[yh, zz] = acc.astype(BF16)
            return 0

        lax.fori_loop(0, RING, gather_last, 0)

    def zpiece(d, half=None, part=None):
        rows = pl.ds(0, 32) if half is None else pl.ds(16 * half, 16)
        which = pl.ds(0, 4) if part is None else pl.ds(2 * part, 2)
        return total.at[which, lax.rem(z + d + RING, RING), rows, :]

    def ypiece(d, half=None, part=None):
        to = lax.rem(y + d + RING, RING)
        rows = pl.ds(32, 32) if half is None else pl.ds(32 + 16 * half, 16)
        which = pl.ds(0, 8) if part is None else pl.ds(4 * part, 4)
        return total.at[to // 2, which, rows, pl.ds(pl.multiple_of(lax.rem(to, 2) * HALF, HALF), HALF)]

    axes = ((zpiece, zdev, za3, za4, zad, zas, zat, 2), (ypiece, ydev, ya3, ya4, yad, yas, yat, 4))
    ways = [(a, side, s) for a in range(2) for side, s in ((0, 1), (1, -1))]
    fours, threes, ones, twos = {}, {}, {}, {}
    for half in range(2):
        for a, side, s in ways:
            piece, dev, b3, b4 = axes[a][:4]
            fours[half, a, side] = remote(piece(4 * s, half, side), b4.at[half, side], dev(2 * s))
            fours[half, a, side].start()
        for a, side, s in ways:
            piece, dev, b3, b4 = axes[a][:4]
            threes[half, a, side] = remote(piece(3 * s, half), b3.at[half, side], dev(s))
            threes[half, a, side].start()
    for a, side, s in ways:
        threes[1, a, side].wait_send()
        ones[a, side] = remote(axes[a][0](s), axes[a][4].at[side], axes[a][1](s))
        ones[a, side].start()
    for half in range(2):
        for a, side, s in ways:
            piece, dev, b3, b4, _, bs, bt, n = axes[a]
            fours[half, a, side].wait_recv()
            threes[half, a, side].wait_recv()
            near, far = pl.ds(n * side, n), pl.ds(n * (1 - side), n)
            mine, third, to = piece(2 * s, half), b3.at[half, side], bt.at[half, side]
            to[near] = (mine[near].astype(F32) + third[near].astype(F32) + b4[half, side].astype(F32)).astype(BF16)
            to[far] = (mine[far].astype(F32) + third[far].astype(F32)).astype(BF16)
            twos[half, a, side] = remote(to, bs.at[half, side], dev(2 * s))
            twos[half, a, side].start()
    last = []
    for a in (1, 0):
        piece, _, _, _, bd, bs, _, _ = axes[a]
        for side in range(2):
            ones[a, side].wait_recv()
            for half in range(2):
                twos[half, a, side].wait_recv()
        halves = []
        for half in range(2):
            rows = pl.ds(16 * half, 16)
            acc = piece(0, half)[...].astype(F32)
            for side in range(2):
                acc = acc + bd[side, :, rows, :].astype(F32) + bs[half, side].astype(F32)
            halves.append(acc)
        done = jnp.concatenate(halves, axis=1).astype(BF16)
        if a == 1:
            pb[...] = done
        else:
            for part in range(2):
                for yh in range(4):
                    pa[2 * yh + part] = done[yh, :, part * HALF:(part + 1) * HALF]
        for d in (4, 3, 5, 2, 6, 1, 7):
            if a == 1:
                copy = remote(pb.at[lax.rem(z + d, RING)], rb.at[d - 1], zdev(d))
            else:
                copy = remote(pa.at[lax.rem(y + d, RING)], ra.at[d - 1], ydev(d))
            copy.start()
            last.append(copy)
    for copy in last:
        copy.wait_recv()
    done_a, done_b = pa[y].astype(F32), pb[z].astype(F32)
    for d in range(RING - 1):
        done_a = done_a + ra[d].astype(F32)
        done_b = done_b + rb[d].astype(F32)
    out[0, 0, pl.ds(0, 32), :] = done_a.astype(BF16)
    out[0, 0, pl.ds(32, 32), :] = done_b.astype(BF16)
    late = [threes[0, a, side] for a, side, _ in ways]
    for copy in list(plain.values()) + list(fours.values()) + late + list(ones.values()) + list(twos.values()) + last:
        copy.wait_send()

    @pl.when(on_up | on_low | relay)
    def _():
        for part in range(2):
            send_on(1, low, part).wait_send()


def on_device(couple, factors, top_reflect, wy_factor, neighbour_ids, kept_rank, merge_map):
    hbm, vmem = (pl.BlockSpec(memory_space=s) for s in (pl.ANY, pltpu.VMEM))
    v = lambda *shape: pltpu.VMEM(shape, BF16)
    return pl.pallas_call(
        kernel,
        name="merge_level",
        out_shape=jax.ShapeDtypeStruct((1, 1, K, HALF), BF16),
        in_specs=[hbm] * 7,
        out_specs=vmem,
        scratch_shapes=[
            pltpu.SMEM((NB, CL), jnp.int32), pltpu.SMEM((CL,), jnp.int32), pltpu.SMEM((NB, CL), jnp.int32),
            v(CL, NB, CW, CW), v(CL, CW, CW), v(CL, K, K), v(CL, K, CW),
            v(CL, HALF, HALF), pltpu.VMEM((CL, HALF), F32), v(2 * CL, HALF, HALF), v(2 * CL, HALF, HALF), pltpu.VMEM((2 * CL, HALF), F32),
            v(NB, CL, K, CW), v(3, CL, K, CW), v(2 * PER, K, CW),
            pltpu.VMEM((2, 8, 128), jnp.int32), pltpu.VMEM((3, 8, 128), jnp.int32), pltpu.SMEM((3, 8, 128), jnp.int32),
            pltpu.VMEM((EMPTY + 1, K, CW), F32), pltpu.VMEM((4, RING, K, CW), F32), v(4, RING, K, CW),
            v(2, 2, 4, 16, CW), v(2, 2, 2, 16, CW), v(2, 4, 32, CW), v(2, 2, 4, 16, CW), v(2, 2, 4, 16, CW),
            v(2, 2, 8, 16, HALF), v(2, 2, 4, 16, HALF), v(2, 8, 32, HALF), v(2, 2, 8, 16, HALF), v(2, 2, 8, 16, HALF),
            v(8, 32, HALF), v(8, 32, HALF), v(7, 32, HALF), v(7, 32, HALF),
            pltpu.SemaphoreType.DMA((13,)), pltpu.SemaphoreType.DMA((SEMS,)), pltpu.SemaphoreType.DMA((SEMS,)),
        ],
        compiler_params=pltpu.CompilerParams(collective_id=0, has_side_effects=True, vmem_limit_bytes=62 << 20),
    )(couple, factors, top_reflect, wy_factor.transpose(0, 2, 1), neighbour_ids.T, kept_rank, merge_map.T)


def solution(mesh):
    own = ("sec", "own", "tile")
    in_specs = (P(own, None, None, None), P(own, None, None), P(own, None, None), P(own, None, None),
                P(own, None), P(own), P(own, None))
    return jax.shard_map(on_device, mesh=mesh, in_specs=in_specs, out_specs=P("sec", "own", None, "tile"), check_vma=False)
```

```python
import jax
import jax.numpy as jnp
from jax import lax
from jax.experimental import pallas as pl
from jax.experimental.pallas import tpu as pltpu
from jax.sharding import PartitionSpec as P

MESH = pl.DeviceIdType.MESH
F32 = jnp.float32
BF16 = jnp.bfloat16
CL, NB, CW, K = 8, 3, 256, 64
HALF = CW // 2
RING = 8
OWNERS = 32
SECTIONS = 8
PER_SECTION = 512
PARTS = 4
PER = CL // PARTS
SEMS = 72
EMPTY = 32


def dot(a, b):
    return lax.dot_general(a, b, (((1,), (0,)), ((), ())), preferred_element_type=F32)


def dot_t(a, b):
    return lax.dot_general(a, b, (((1,), (1,)), ((), ())), preferred_element_type=F32)


def kernel(couple, factors, reflect, wy, nid_h, rank_h, mmap_h, out,
           nid, rank, mmap, couple_v, fac, refl_v, wy_v, pack, diag, sec_b, sec_u, sec_d, zs, zr, fw, tab_s, tab_v, tab, coarse, part_total, total,
           za3, za4, zad, zas, zat, ya3, ya4, yad, yas, yat, pa, pb, ra, rb,
           load_sem, ss, rs):
    sec, own, tile = lax.axis_index("sec"), lax.axis_index("own"), lax.axis_index("tile")
    z, y = lax.rem(own, RING), (own // RING) * 2 + tile

    def zdev(d):
        return {"own": (own // RING) * RING + lax.rem(z + d + RING, RING)}

    def ydev(d):
        to = lax.rem(y + d + RING, RING)
        return {"own": (to // 2) * RING + z, "tile": lax.rem(to, 2)}

    def sdev(d):
        return {"sec": lax.rem(sec + d + SECTIONS, SECTIONS)}

    has_low, has_up = own > 0, own < OWNERS - 1
    low = jnp.where(has_low, own - 1, own + 1)
    up = jnp.where(has_up, own + 1, own - 1)

    ints = [pltpu.make_async_copy(a, b, load_sem.at[6 + i]) for i, (a, b) in enumerate(((mmap_h, mmap), (nid_h, nid), (rank_h, rank)))]
    loads = [pltpu.make_async_copy(factors, fac, load_sem.at[0]),
             pltpu.make_async_copy(wy, wy_v, load_sem.at[1]),
             pltpu.make_async_copy(reflect, refl_v, load_sem.at[2])]
    couples = []
    for part in range(PARTS):
        at = pl.ds(part * PER, PER)
        couples.append(pltpu.make_async_copy(couple.at[at], couple_v.at[at], load_sem.at[9 + part]))
    for copy in ints + loads + couples:
        copy.start()

    barrier = pltpu.get_barrier_semaphore()

    def greet(to):
        pl.semaphore_signal(barrier, inc=1, device_id=to, device_id_type=MESH)

    greet(sdev(1))
    greet(sdev(-1))

    @pl.when(has_low)
    def _():
        greet({"own": own - 1})

    @pl.when(has_up)
    def _():
        greet({"own": own + 1})

    for d in (2, -2, 1, -1):
        greet(zdev(d))
        greet(ydev(d))

    at_start = own == 0
    at_end = own == OWNERS - 1
    for_start = ((own == 25) & (tile == 1)) | ((own == 9) & (tile == 0))
    relay = ((own == 22) & (tile == 1)) | ((own == 6) & (tile == 0)) | for_start
    relay_dev = {"own": jnp.where(at_start, jnp.where(tile == 0, 25, 9), jnp.where(tile == 0, 22, 6)), "tile": 1 - tile}
    relay_from = jnp.where(for_start, 0, OWNERS - 1)
    relay_to = jnp.where(for_start, 1, OWNERS - 2)

    @pl.when(at_start | at_end)
    def _():
        greet(relay_dev)

    @pl.when(relay)
    def _():
        greet({"own": relay_from, "tile": 1 - tile})

    met = 2 + 8 + has_low.astype(jnp.int32) + has_up.astype(jnp.int32) + (at_start | at_end | relay).astype(jnp.int32)
    early = z < RING // 2
    late = z >= RING // 2

    count = [0]

    def remote(src, dst, to):
        i = count[0]
        count[0] += 1
        return pltpu.make_async_remote_copy(src_ref=src, dst_ref=dst, send_sem=ss.at[i], recv_sem=rs.at[i],
                                            device_id=to, device_id_type=MESH)

    blocks, squares = [], []
    for side, d in ((0, 1), (1, -1)):
        at = pl.ds(side * CL, CL)
        blocks.append(remote(fac.at[:, pl.ds(HALF, HALF), pl.ds(0, HALF)], sec_b.at[at], sdev(d)))
        squares += [remote(pack, sec_u.at[at], sdev(d)), remote(diag, sec_d.at[at], sdev(d))]
    sec_copies = blocks + squares
    sq_r = lax.broadcasted_iota(jnp.int32, (HALF, HALF), 0)
    sq_c = lax.broadcasted_iota(jnp.int32, (HALF, HALF), 1)

    def open_up():
        pl.semaphore_wait(barrier, met)
        for copy in blocks:
            copy.start()

    def pack_up():
        for c in range(CL):
            lower = fac[c, pl.ds(HALF, HALF), pl.ds(HALF, HALF)].astype(F32)
            diag[pl.ds(c, 1), :] = jnp.sum(jnp.where(sq_r == sq_c, lower, 0.0), axis=0, keepdims=True)
            upper = fac[c, pl.ds(0, HALF), pl.ds(0, HALF)].astype(F32)
            pack[c] = jnp.where(sq_r >= sq_c, upper, lower.T).astype(BF16)

    base_sem = count[0]
    count[0] += 3 * PARTS
    fw_sem = count[0]
    count[0] += 2
    on_sem = count[0]
    count[0] += 2
    for copy in loads + ints:
        copy.wait()
    r_iota = lax.broadcasted_iota(jnp.int32, (K, CW), 0)
    c_iota = lax.broadcasted_iota(jnp.int32, (K, CW), 1)
    eye = jnp.where(r_iota == c_iota, 1.0, 0.0)
    low_group = jnp.where(has_low, 0, 2)
    up_group = jnp.where(has_up, 1, 2)
    cross_low = (z == 0) & has_low
    cross_up = (z == RING - 1) & has_up
    tops = []
    for c in range(CL):
        t = eye - dot(refl_v[c], wy_v[c])
        t = jnp.where(r_iota < rank[c], t, 0.0).astype(BF16)
        tops.append(dot(t, fac[c]).astype(BF16))
    plain, by_way, by_relay = {}, {}, {}
    for part in range(PARTS):
        at = pl.ds(part * PER, PER)
        for j in range(2):
            group = (low_group, up_group)[j]
            plain[j, part] = pltpu.make_async_remote_copy(
                src_ref=zs.at[j, at], dst_ref=zr.at[group, at], send_sem=ss.at[base_sem + j * PARTS + part],
                recv_sem=rs.at[base_sem + group * PARTS + part], device_id={"own": (low, up)[j]}, device_id_type=MESH)
            if part < 2:
                by_way[j, part] = pltpu.make_async_remote_copy(
                    src_ref=zs.at[j, at], dst_ref=fw.at[at], send_sem=ss.at[base_sem + j * PARTS + part],
                    recv_sem=rs.at[fw_sem + part], device_id=zdev((-1, 1)[j]), device_id_type=MESH)
                by_relay[j, part] = pltpu.make_async_remote_copy(
                    src_ref=zs.at[j, at], dst_ref=fw.at[at], send_sem=ss.at[base_sem + j * PARTS + part],
                    recv_sem=rs.at[fw_sem + part], device_id=relay_dev, device_id_type=MESH)

    def z_send(part):
        for j in (1, 0):
            if part >= 2:
                plain[j, part].start()
                continue
            crossing = (cross_low, cross_up)[j]

            @pl.when(crossing)
            def _():
                by_way[j, part].start()

            doubled = (at_start, at_end)[j]

            @pl.when(doubled)
            def _():
                by_relay[j, part].start()

            crossing = crossing | doubled

            @pl.when(jnp.logical_not(crossing))
            def _():
                plain[j, part].start()

    lane = lax.broadcasted_iota(jnp.int32, (8, 128), 1)
    row = lax.broadcasted_iota(jnp.int32, (8, 128), 0)

    def table(groups):
        first = jnp.full((8, 128), EMPTY, jnp.int32)
        second = jnp.full((8, 128), EMPTY, jnp.int32)
        local = jnp.zeros((8, 128), jnp.int32)
        for j, base, wanted in groups:
            for c in range(CL):
                hit = lane == mmap[j, c]
                if wanted is not None:
                    hit = hit & wanted
                second = jnp.where(hit & (first != EMPTY), base + c, second)
                first = jnp.where(hit & (first == EMPTY), base + c, first)
                local = jnp.where(lane == base + c, nid[j, c] & (CL - 1), local)
        return jnp.where(row == 0, first, jnp.where(row == 1, second, local))

    at_low_end = jnp.full((8, 128), own, jnp.int32) == 0
    at_up_end = jnp.full((8, 128), own, jnp.int32) == OWNERS - 1
    to_low = remote(tab_s.at[0], tab_v.at[1], {"own": low})
    to_up = remote(tab_s.at[1], tab_v.at[0], {"own": up})

    def fill_tables():
        tab_s[0] = table([(0, 8, None), (1, 24, at_up_end)])
        tab_s[1] = table([(1, 16, None), (0, 24, at_low_end)])
        tab_v[2] = table([(2, 0, None)])
        nothing = jnp.where(row < 2, EMPTY, 0)

        @pl.when(jnp.logical_not(has_low))
        def _():
            tab_v[0] = nothing

        @pl.when(jnp.logical_not(has_up))
        def _():
            tab_v[1] = nothing

        coarse[EMPTY] = jnp.zeros((K, CW), F32)

    def send_tables():
        @pl.when(has_low)
        def _():
            to_low.start()

        @pl.when(has_up)
        def _():
            to_up.start()

    @pl.when(early)
    def _():
        fill_tables()
        pack_up()

    for part in range(PARTS):
        couples[part].wait()
        for j in (1, 0, 2):
            for c in range(part * PER, part * PER + PER):
                zs[j, c] = dot(tops[c], couple_v[c, j]).astype(BF16)

        @pl.when(late)
        def _():
            if part == 0:
                open_up()
            z_send(part)

    @pl.when(early)
    def _():
        open_up()
        for part in range(PARTS):
            z_send(part)
        send_tables()

    @pl.when(late)
    def _():
        fill_tables()
        send_tables()
        pack_up()

    for copy in squares:
        copy.start()

    def send_on(group, to, part):
        at = pl.ds(part * PER, PER)
        return pltpu.make_async_remote_copy(
            src_ref=fw.at[at], dst_ref=zr.at[group, at], send_sem=ss.at[on_sem + part],
            recv_sem=rs.at[base_sem + group * PARTS + part], device_id={"own": to}, device_id_type=MESH)

    def fw_landed(part):
        at = pl.ds(part * PER, PER)
        pltpu.make_async_remote_copy(src_ref=zs.at[0, at], dst_ref=fw.at[at], send_sem=ss.at[base_sem], recv_sem=rs.at[fw_sem + part],
                                     device_id=zdev(1), device_id_type=MESH).wait_recv()

    def landed(group, part):
        at = pl.ds(part * PER, PER)
        pltpu.make_async_remote_copy(
            src_ref=zs.at[0, at], dst_ref=zr.at[group, at], send_sem=ss.at[base_sem], recv_sem=rs.at[base_sem + group * PARTS + part],
            device_id={"own": low}, device_id_type=MESH).wait_recv()

    on_up = (z == 0) & (own < OWNERS - RING)
    on_low = (z == RING - 1) & (own >= RING)
    for part in range(2):
        @pl.when(on_up)
        def _():
            fw_landed(part)
            send_on(1, own + RING, part).start()

        @pl.when(on_low)
        def _():
            fw_landed(part)
            send_on(0, own - RING, part).start()

        @pl.when(relay)
        def _():
            fw_landed(part)
            pltpu.make_async_remote_copy(
                src_ref=fw.at[pl.ds(part * PER, PER)], dst_ref=zr.at[2, pl.ds(part * PER, PER)], send_sem=ss.at[on_sem + part],
                recv_sem=rs.at[base_sem + 2 * PARTS + part], device_id={"own": relay_to, "tile": 1 - tile}, device_id_type=MESH).start()

    @pl.when(has_low)
    def _():
        to_low.wait_send()
        to_up_like = to_up
        to_up_like.wait_recv()

    @pl.when(has_up)
    def _():
        to_up.wait_send()
        to_low.wait_recv()

    tab_copy = pltpu.make_async_copy(tab_v, tab, load_sem.at[5])
    tab_copy.start()
    tab_copy.wait()

    for copy in sec_copies:
        copy.wait()
    for c in range(CL):
        n = nid[2, c]
        at = (n & (CL - 1)) + jnp.where(n // PER_SECTION > sec, CL, 0)
        square = sec_u[at].astype(F32)
        line = sec_d[pl.ds(at, 1), :]
        head = jnp.where(sq_r >= sq_c, square, 0.0).astype(BF16)
        tail = jnp.where(sq_r < sq_c, square, jnp.where(sq_r == sq_c, line, 0.0)).astype(BF16)
        near, far = zs[2, c, :, pl.ds(0, HALF)], zs[2, c, :, pl.ds(HALF, HALF)]
        coarse[c, :, pl.ds(0, HALF)] = dot_t(near, head)
        coarse[c, :, pl.ds(HALF, HALF)] = dot_t(near, sec_b[at]) + dot(far, tail)

    def finish(group, base, side, part):
        for c in range(part * PER, part * PER + PER):
            at = tab[side, 2, base + c]
            coarse[base + c] = dot_t(zr[group, c], fac[at])

    def take(group, base, side):
        for part in range(PARTS):
            landed(group, part)
        for part in range(PARTS):
            finish(group, base, side, part)

    up_last = z >= RING - 2
    side_first = jnp.where(up_last, 0, 1)
    side_last = 1 - side_first

    @pl.when(jnp.logical_not(up_last))
    def _():
        take(0, 8, 1)

    @pl.when(up_last)
    def _():
        take(1, 16, 0)

    for yh in range(4):
        def gather(zz, _):
            m = yh * RING + zz
            acc = coarse[tab[2, 0, m]] + coarse[tab[2, 1, m]]
            part_total[yh, zz] = acc + coarse[tab[side_first, 0, m]] + coarse[tab[side_first, 1, m]]
            return 0

        lax.fori_loop(0, RING, gather, 0)

    @pl.when(jnp.logical_not(up_last) & has_low)
    def _():
        take(1, 16, 0)

    @pl.when(up_last & has_up)
    def _():
        take(0, 8, 1)

    @pl.when(own == 1)
    def _():
        take(2, 24, 0)

    @pl.when(own == OWNERS - 2)
    def _():
        take(2, 24, 1)

    for yh in range(4):
        def gather_last(zz, _):
            m = yh * RING + zz
            acc = part_total[yh, zz] + coarse[tab[side_last, 0, m]] + coarse[tab[side_last, 1, m]]
            total[yh, zz] = acc.astype(BF16)
            return 0

        lax.fori_loop(0, RING, gather_last, 0)

    def zpiece(d, half=None, part=None):
        rows = pl.ds(0, 32) if half is None else pl.ds(16 * half, 16)
        which = pl.ds(0, 4) if part is None else pl.ds(2 * part, 2)
        return total.at[which, lax.rem(z + d + RING, RING), rows, :]

    def ypiece(d, half=None, part=None):
        to = lax.rem(y + d + RING, RING)
        rows = pl.ds(32, 32) if half is None else pl.ds(32 + 16 * half, 16)
        which = pl.ds(0, 8) if part is None else pl.ds(4 * part, 4)
        return total.at[to // 2, which, rows, pl.ds(pl.multiple_of(lax.rem(to, 2) * HALF, HALF), HALF)]

    axes = ((zpiece, zdev, za3, za4, zad, zas, zat, 2), (ypiece, ydev, ya3, ya4, yad, yas, yat, 4))
    ways = [(a, side, s) for a in (1, 0) for side, s in ((0, 1), (1, -1))]
    fours, threes, ones, twos = {}, {}, {}, {}
    for half in range(2):
        for a, side, s in ways:
            piece, dev, b3, b4 = axes[a][:4]
            fours[half, a, side] = remote(piece(4 * s, half, side), b4.at[half, side], dev(2 * s))
            fours[half, a, side].start()
        for a, side, s in ways:
            piece, dev, b3, b4 = axes[a][:4]
            threes[half, a, side] = remote(piece(3 * s, half), b3.at[half, side], dev(s))
            threes[half, a, side].start()
    for a, side, s in ways:
        threes[1, a, side].wait_send()
        ones[a, side] = remote(axes[a][0](s), axes[a][4].at[side], axes[a][1](s))
        ones[a, side].start()
    for half in range(2):
        for a, side, s in ways:
            piece, dev, b3, b4, _, bs, bt, n = axes[a]
            fours[half, a, side].wait_recv()
            threes[half, a, side].wait_recv()
            near, far = pl.ds(n * side, n), pl.ds(n * (1 - side), n)
            mine, third, to = piece(2 * s, half), b3.at[half, side], bt.at[half, side]
            to[near] = (mine[near].astype(F32) + third[near].astype(F32) + b4[half, side].astype(F32)).astype(BF16)
            to[far] = (mine[far].astype(F32) + third[far].astype(F32)).astype(BF16)
            twos[half, a, side] = remote(to, bs.at[half, side], dev(2 * s))
            twos[half, a, side].start()
    last = []
    for a in (1, 0):
        piece, _, _, _, bd, bs, _, _ = axes[a]
        for side in range(2):
            ones[a, side].wait_recv()
            for half in range(2):
                twos[half, a, side].wait_recv()
        halves = []
        for half in range(2):
            rows = pl.ds(16 * half, 16)
            acc = piece(0, half)[...].astype(F32)
            for side in range(2):
                acc = acc + bd[side, :, rows, :].astype(F32) + bs[half, side].astype(F32)
            halves.append(acc)
        done = jnp.concatenate(halves, axis=1).astype(BF16)
        if a == 1:
            pb[...] = done
        else:
            for part in range(2):
                for yh in range(4):
                    pa[2 * yh + part] = done[yh, :, part * HALF:(part + 1) * HALF]
        for d in (4, 3, 5, 2, 6, 1, 7):
            if a == 1:
                copy = remote(pb.at[lax.rem(z + d, RING)], rb.at[d - 1], zdev(d))
            else:
                copy = remote(pa.at[lax.rem(y + d, RING)], ra.at[d - 1], ydev(d))
            copy.start()
            last.append(copy)
    for copy in last:
        copy.wait_recv()
    done_a, done_b = pa[y].astype(F32), pb[z].astype(F32)
    for d in range(RING - 1):
        done_a = done_a + ra[d].astype(F32)
        done_b = done_b + rb[d].astype(F32)
    out[0, 0, pl.ds(0, 32), :] = done_a.astype(BF16)
    out[0, 0, pl.ds(32, 32), :] = done_b.astype(BF16)
    late = [threes[0, a, side] for a, side, _ in ways]
    for copy in list(plain.values()) + list(fours.values()) + late + list(ones.values()) + list(twos.values()) + last:
        copy.wait_send()

    @pl.when(on_up | on_low | relay)
    def _():
        for part in range(2):
            send_on(1, low, part).wait_send()


def on_device(couple, factors, top_reflect, wy_factor, neighbour_ids, kept_rank, merge_map):
    hbm, vmem = (pl.BlockSpec(memory_space=s) for s in (pl.ANY, pltpu.VMEM))
    v = lambda *shape: pltpu.VMEM(shape, BF16)
    return pl.pallas_call(
        kernel,
        name="merge_level",
        out_shape=jax.ShapeDtypeStruct((1, 1, K, HALF), BF16),
        in_specs=[hbm] * 7,
        out_specs=vmem,
        scratch_shapes=[
            pltpu.SMEM((NB, CL), jnp.int32), pltpu.SMEM((CL,), jnp.int32), pltpu.SMEM((NB, CL), jnp.int32),
            v(CL, NB, CW, CW), v(CL, CW, CW), v(CL, K, K), v(CL, K, CW),
            v(CL, HALF, HALF), pltpu.VMEM((CL, HALF), F32), v(2 * CL, HALF, HALF), v(2 * CL, HALF, HALF), pltpu.VMEM((2 * CL, HALF), F32),
            v(NB, CL, K, CW), v(3, CL, K, CW), v(2 * PER, K, CW),
            pltpu.VMEM((2, 8, 128), jnp.int32), pltpu.VMEM((3, 8, 128), jnp.int32), pltpu.SMEM((3, 8, 128), jnp.int32),
            pltpu.VMEM((EMPTY + 1, K, CW), F32), pltpu.VMEM((4, RING, K, CW), F32), v(4, RING, K, CW),
            v(2, 2, 4, 16, CW), v(2, 2, 2, 16, CW), v(2, 4, 32, CW), v(2, 2, 4, 16, CW), v(2, 2, 4, 16, CW),
            v(2, 2, 8, 16, HALF), v(2, 2, 4, 16, HALF), v(2, 8, 32, HALF), v(2, 2, 8, 16, HALF), v(2, 2, 8, 16, HALF),
            v(8, 32, HALF), v(8, 32, HALF), v(7, 32, HALF), v(7, 32, HALF),
            pltpu.SemaphoreType.DMA((13,)), pltpu.SemaphoreType.DMA((SEMS,)), pltpu.SemaphoreType.DMA((SEMS,)),
        ],
        compiler_params=pltpu.CompilerParams(collective_id=0, has_side_effects=True, vmem_limit_bytes=62 << 20),
    )(couple, factors, top_reflect, wy_factor.transpose(0, 2, 1), neighbour_ids.T, kept_rank, merge_map.T)


def solution(mesh):
    own = ("sec", "own", "tile")
    in_specs = (P(own, None, None, None), P(own, None, None), P(own, None, None), P(own, None, None),
                P(own, None), P(own), P(own, None))
    return jax.shard_map(on_device, mesh=mesh, in_specs=in_specs, out_specs=P("sec", "own", None, "tile"), check_vma=False)
```
